512 devices in a mesh: expert: 32 (over y, z_lo), dp: 4 (over x), tensor: 4 (over z_hi, core).
Axes of the slice: x: 4, y: 4, z: 16 (z_hi: 2, z_lo: 8; z = z_hi * 8 + z_lo), core: 2. Of those that a mesh axis runs over, the one named last changes fastest.
Arguments:
- tokens: bfloat16 [16384, 1664], P(('expert', 'dp')), may hold values from -6 to 6
- grad_out: bfloat16 [16384, 1664], P(('expert', 'dp')), may hold values from -6 to 6
- picks: int32 [128, 32, 8], P(('expert', 'dp')), may hold values from 0 to 127, as said below
- gates: bfloat16 [128, 32, 8], P(('expert', 'dp')), may hold values from 0.19921875 to 1
- w_in: bfloat16 [32, 1664, 4096], P('expert', 'dp', 'tensor'), may hold values from -0.15625 to 0.15625
- w_out: bfloat16 [32, 4096, 1664], P('expert', 'tensor', 'dp'), may hold values from -0.09375 to 0.09375
- scale_in: float32 [32, 4096], P('expert', 'tensor'), may hold values from 0.012 to 0.06
- scale_out: float32 [32, 1664], P('expert', 'dp'), may hold values from 0.008 to 0.04
Outputs:
- grad_tokens: bfloat16 [16384, 1664], P(('expert', 'dp'), 'tensor')
- grad_gates: float32 [128, 32, 8], P(('expert', 'dp'))
- grad_w_in: bfloat16 [32, 1664, 4096], P('expert', 'dp', 'tensor')
- grad_w_out: bfloat16 [32, 4096, 1664], P('expert', 'tensor', 'dp')
- grad_scale_in: float32 [32, 4096], P('expert', 'tensor')
- grad_scale_out: float32 [32, 1664], P('expert', 'dp')
The draws below stay inside these ranges and needn't reach their ends.
Inputs may be any that keep to these rules, and one draw needn't show every extreme that they name: `picks`: for each token shard and expert the 8 entries are distinct rows of that shard, counted within its 128 tokens.
All inputs are finite; a program needn't handle non-finite values.
Results may differ from the reference program's by a relative error of at most 0.0075.
Values may be sent and summed in bfloat16 or wider, within the bound.
A program may use at most 64 MiB of HBM per device.

```python
import math
import jax
import jax.numpy as jnp
from jax import lax

D = 1664
FF = 4096
TOK_DEV = 128
EXPERTS = 32
PICKS = 8
SHARDS = 128
TOKENS = 16384


def draw_picks(key, part):
    key = jax.random.fold_in(key, 7)
    scores = jax.random.randint(key, (SHARDS, EXPERTS, TOK_DEV), 0, 1 << 20)
    scores = scores * TOK_DEV + jnp.arange(TOK_DEV, dtype=jnp.int32)
    ranked = jnp.argsort(scores, axis=-1)
    return ranked[:, :, :PICKS].astype(jnp.int32)


def level_of(own_key, extent, shards, low, high):
    factor_of, own = 1.0, jax.random.fold_in(own_key, 6)
    for position, shards_of in shards:
        steps = jnp.exp(jax.random.uniform(jax.random.fold_in(own, position), (shards_of,), jnp.float32, low / len(shards), high / len(shards)))
        factor_of = factor_of * jnp.repeat(steps, extent[position] // shards_of).reshape([-1 if axis == position else 1 for axis in range(len(extent))])
    return factor_of


def noise(rng, shape, deviation, most, split=(), held_as=jnp.bfloat16):
    result = deviation * jax.random.normal(rng, shape, jnp.float32)
    if split:
        result = result * level_of(rng, shape, split, -0.22, 0.18)
    return jnp.clip(result, -most, most).astype(held_as)


def setup_inputs(seed: int = 0) -> dict:
    key_list = jax.random.split(jax.random.key(seed), 9)
    tokens = noise(key_list[0], (TOKENS, D), 1.0, 6.0, ((0, 128),))
    grad_out = noise(key_list[1], (TOKENS, D), 1.0, 6.0, ((0, 128),))
    picks = draw_picks(jax.random.fold_in(key_list[8], 71), 0)
    gates = jnp.clip(0.19921875 + 0.80078125 * jax.random.uniform(key_list[3], (SHARDS, EXPERTS, PICKS), jnp.float32) ** level_of(key_list[3], (SHARDS, EXPERTS, PICKS), ((0, 128),), -0.2, 0.2), 0.19921875, 1.0).astype(jnp.bfloat16)
    w_in = noise(key_list[4], (EXPERTS, D, FF), D ** -0.5, 0.15625, ((0, 32), (1, 4), (2, 4)))
    w_out = noise(key_list[5], (EXPERTS, FF, D), FF ** -0.5, 0.09375, ((0, 32), (1, 4), (2, 4)))
    scale_in = jnp.clip(jnp.exp(math.log(0.06) - 1.60943788 * jax.random.uniform(key_list[6], (EXPERTS, FF), jnp.float32) ** level_of(key_list[6], (EXPERTS, FF), ((0, 32), (1, 4)), -0.2, 0.2)), 0.012, 0.06)
    scale_out = jnp.clip(jnp.exp(math.log(0.04) - 1.6094378 * jax.random.uniform(key_list[7], (EXPERTS, D), jnp.float32) ** level_of(key_list[7], (EXPERTS, D), ((0, 32), (1, 4)), -0.2, 0.2)), 0.008, 0.04)
    return {"tokens": tokens, "grad_out": grad_out, "picks": picks, "gates": gates, "w_in": w_in, "w_out": w_out, "scale_in": scale_in, "scale_out": scale_out}


gelu_coeff = 0.7978845608028654
cubic_coeff = 0.044715


def soft_clip(weight, channel_scale):
    scaled = weight.astype(jnp.float32) / channel_scale
    tangent = jnp.tanh(scaled)
    return channel_scale * tangent, tangent, scaled


def gelu_parts(hidden):
    inner_arg = gelu_coeff * (hidden + cubic_coeff * hidden * hidden * hidden)
    tangent = jnp.tanh(inner_arg)
    output = 0.5 * hidden * (1.0 + tangent)
    gelu_slope = 0.5 * (1.0 + tangent) + 0.5 * hidden * (1.0 - tangent * tangent) * gelu_coeff * (1.0 + 3.0 * cubic_coeff * hidden * hidden)
    return output, gelu_slope


def reference(tokens, grad_out, picks, gates, w_in, w_out, scale_in, scale_out):
    slot_total = SHARDS * PICKS
    factor = slot_total ** -0.5
    offsets = jnp.arange(SHARDS, dtype=jnp.int32) * TOK_DEV
    flat_rows = (picks + offsets[:, None, None]).astype(jnp.int32)

    def one_expert(grad_sum, expert_id):
        row_index = lax.dynamic_index_in_dim(flat_rows, expert_id, 1, False).reshape(-1)
        slot_gates = lax.dynamic_index_in_dim(gates, expert_id, 1, False).reshape(-1, 1).astype(jnp.float32)
        weight_in = lax.dynamic_index_in_dim(w_in, expert_id, 0, False)
        weight_out = lax.dynamic_index_in_dim(w_out, expert_id, 0, False)
        row_in = lax.dynamic_index_in_dim(scale_in, expert_id, 0, False)
        row_out = lax.dynamic_index_in_dim(scale_out, expert_id, 0, False)
        quant_in, tangent_in, scaled_in = soft_clip(weight_in, row_in[None, :])
        quant_out, tangent_out, scaled_out = soft_clip(weight_out, row_out[None, :])
        quant_in = quant_in.astype(jnp.bfloat16)
        quant_out = quant_out.astype(jnp.bfloat16)
        picked = tokens[row_index]
        picked_grad = grad_out[row_index]
        hidden = jnp.dot(picked, quant_in, preferred_element_type=jnp.float32)
        act_value, gelu_slope = gelu_parts(hidden)
        activation = act_value.astype(jnp.bfloat16)
        back_prop = jnp.dot(picked_grad, quant_out.T, preferred_element_type=jnp.float32)
        gate_grad = jnp.sum(activation.astype(jnp.float32) * back_prop, axis=1)
        hidden_grad = (slot_gates * back_prop * gelu_slope).astype(jnp.bfloat16)
        out_grad = (slot_gates * picked_grad.astype(jnp.float32)).astype(jnp.bfloat16)
        total_in = jnp.dot(picked.T, hidden_grad, preferred_element_type=jnp.float32) * factor
        total_out = jnp.dot(activation.T, out_grad, preferred_element_type=jnp.float32) * factor
        sech_in = 1.0 - tangent_in * tangent_in
        sech_out = 1.0 - tangent_out * tangent_out
        grad_win = (total_in * sech_in).astype(jnp.bfloat16)
        grad_wout = (total_out * sech_out).astype(jnp.bfloat16)
        grad_sin = jnp.sum(total_in * (tangent_in - scaled_in * sech_in), axis=0)
        grad_sout = jnp.sum(total_out * (tangent_out - scaled_out * sech_out), axis=0)
        token_grad = jnp.dot(hidden_grad, quant_in.T, preferred_element_type=jnp.float32)
        grad_sum = grad_sum.at[row_index].add(token_grad)
        return grad_sum, (gate_grad.reshape(SHARDS, PICKS), grad_win, grad_wout, grad_sin, grad_sout)

    zero_grads = jnp.zeros((TOKENS, D), jnp.float32)
    summed, stacked = lax.scan(one_expert, zero_grads, jnp.arange(EXPERTS, dtype=jnp.int32))
    gate_all = jnp.transpose(stacked[0], (1, 0, 2))
    return (summed.astype(jnp.bfloat16), gate_all, stacked[1], stacked[2], stacked[3], stacked[4])
```

```python
import functools

import jax
import jax.numpy as jnp
from jax import lax
from jax.experimental import pallas as pl
from jax.experimental.pallas import tpu as pltpu
from jax.sharding import PartitionSpec as P

gelu_coeff = 0.7978845608028654
cubic_coeff = 0.044715

D = 1664
HALF = 896
MIB = 1 << 20
f32, bf16 = jnp.float32, jnp.bfloat16
VMEM = pl.BlockSpec(memory_space=pltpu.VMEM)
ANY = pl.BlockSpec(memory_space=pl.ANY)
GROUPS = (0, 1, 7, 2, 6, 3, 5, 4)


def where_am_i():
    e, d, t = lax.axis_index("expert"), lax.axis_index("dp"), lax.axis_index("tensor")
    y, zl = lax.div(e, 8), lax.rem(e, 8)
    zh, c = lax.div(t, 2), lax.rem(t, 2)
    return e, d, t, y, zl, zh, c


def neighbours():
    e, d, t, y, zl, zh, c = where_am_i()
    z = zh * 8 + zl

    def at(dy, dz):
        yy, zz = lax.rem(y + dy + 4, 4), lax.rem(z + dz + 16, 16)
        return (yy * 8 + lax.rem(zz, 8), d, lax.div(zz, 8) * 2 + c)

    def along(dx):
        return (e, lax.rem(d + dx, 4), t)

    return at, along, (e, d, t + 1 - 2 * c)


def greet(devices):
    barrier = pltpu.get_barrier_semaphore()
    for device in devices:
        pl.semaphore_signal(barrier, inc=1, device_id=device, device_id_type=pl.DeviceIdType.MESH)
    pl.semaphore_wait(barrier, len(devices))


def remote(src, dst, send, recv, device):
    return pltpu.make_async_remote_copy(
        src_ref=src, dst_ref=dst, send_sem=send, recv_sem=recv,
        device_id=device, device_id_type=pl.DeviceIdType.MESH,
    )


def bring_in(
    tokens, grads, picks, gates, w_in, w_out, s_out,
    xg, win, wout, so,
    stage, local_sem, w_send, w_recv, a_send, a_recv, x_send, x_recv, f_send, f_recv, p_send, p_recv,
):
    e, d, t, y, zl, zh, c = where_am_i()
    at, along, partner = neighbours()
    greet(
        [at(dy, dz) for dz in range(-4, 5) for dy in range(4) if (dy, dz) != (0, 0)]
        + [along(dx) for dx in (1, 2, 3)]
        + [partner]
    )
    w_copies = []
    for dx in (1, 3, 2):
        there = lax.rem(d + dx, 4)
        cols = pl.ds(pl.multiple_of(there * 256, 256), 256)
        for k, (src, dst) in enumerate(
            ((w_in.at[:, cols], win.at[d]), (w_out.at[cols, :], wout.at[d]), (s_out, so.at[d]))
        ):
            copy = remote(src, dst, w_send.at[k, dx - 1], w_recv.at[k, dx - 1], along(dx))
            copy.start()
            w_copies.append(copy)
    mine = pl.ds(pl.multiple_of(d * 256, 256), 256)
    locals_ = [
        pltpu.make_async_copy(w_in.at[:, mine], win.at[d], local_sem.at[0]),
        pltpu.make_async_copy(w_out.at[mine, :], wout.at[d], local_sem.at[1]),
        pltpu.make_async_copy(s_out, so.at[d], local_sem.at[2]),
    ]
    for copy in locals_:
        copy.start()

    onehot = (lax.broadcasted_iota(jnp.int32, (256, 128), 1) == picks[...]).astype(bf16)
    body = pl.ds(pl.multiple_of(c * HALF, 128), HALF - 128)
    gate_tile = jnp.broadcast_to(gates[...], (256, 128))

    def rows(ref):
        most = jnp.dot(onehot, ref[:, body], preferred_element_type=f32)
        last = jnp.dot(onehot, ref[:, HALF - 128 : HALF], preferred_element_type=f32)
        last = jnp.where(c == 0, last, gate_tile)
        return most.reshape(32, 8, HALF - 128), last.reshape(32, 8, 128)

    x_most, x_last = rows(tokens)
    g_most, g_last = rows(grads)
    stage[:, :, 0 : HALF - 128] = jnp.concatenate([x_most, g_most], axis=1).astype(bf16)
    stage[:, :, HALF - 128 : HALF] = jnp.concatenate([x_last, g_last], axis=1).astype(bf16)

    own = pltpu.make_async_copy(stage.at[e], xg.at[0, c, 0], local_sem.at[3])
    own.start()
    for dz in GROUPS:
        for dy in range(4):
            if (dy, dz) == (0, 0):
                continue
            way = dz if dz < 4 else dz - 8
            if dz == 4:
                way = 4 if dy < 2 else -4
            device = at(dy, way)
            remote(
                stage.at[device[0]], xg.at[0, c, dz * 4 + dy], a_send.at[dz], a_recv.at[dz], device
            ).start()

    def part(block, g):
        return xg.at[block, c, pl.ds(4 * g, 4)]

    def to_partner(block, g):
        return remote(part(block, g), part(block, g), p_send.at[block, g], p_recv.at[block, g], partner)

    def forth(g):
        return remote(part(0, g), part(1, g), x_send.at[0, g], x_recv.at[0, g], along(1))

    def back(g):
        return remote(part(0, g), part(3, g), x_send.at[1, g], x_recv.at[1, g], along(3))

    def onward(g):
        if GROUPS.index(g) % 2 == 0:
            return remote(part(1, g), part(2, g), f_send.at[g], f_recv.at[g], along(1))
        return remote(part(3, g), part(2, g), f_send.at[g], f_recv.at[g], along(3))

    def arrived(g):
        n = 3 if g == 0 else 4
        ref = xg.at[0, c, pl.ds(4 * g + 4 - n, n)]
        return remote(ref, ref, a_send.at[g], a_recv.at[g], partner)

    own.wait()
    for step in range(8 + 4):
        if step < 8:
            g = GROUPS[step]
            arrived(g).wait_recv()
            forth(g).start()
            back(g).start()
            to_partner(0, g).start()
        if 2 <= step < 10:
            g = GROUPS[step - 2]
            forth(g).wait_recv()
            back(g).wait_recv()
            onward(g).start()
            to_partner(1, g).start()
            to_partner(3, g).start()
        if 4 <= step:
            g = GROUPS[step - 4]
            onward(g).wait_recv()
            to_partner(2, g).start()
    for g in GROUPS:
        arrived(g).wait_send()
        forth(g).wait_send()
        back(g).wait_send()
        onward(g).wait_send()
        for block in range(4):
            to_partner(block, g).wait()
    for copy in locals_ + w_copies:
        copy.wait()


def gelu_parts(hidden):
    inner_arg = gelu_coeff * (hidden + cubic_coeff * hidden * hidden * hidden)
    tangent = jnp.tanh(inner_arg)
    output = 0.5 * hidden * (1.0 + tangent)
    gelu_slope = 0.5 * (1.0 + tangent) + 0.5 * hidden * (1.0 - tangent * tangent) * gelu_coeff * (
        1.0 + 3.0 * cubic_coeff * hidden * hidden
    )
    return output, gelu_slope


def spread(ref, rows):
    pieces = []
    for d in range(4):
        wide = jnp.concatenate([ref[d].astype(f32), jnp.zeros((rows, 96), f32)], axis=1)
        pieces.append(pltpu.roll(wide, 32 * d, 1) if d else wide)
    out = []
    for d in range(4):
        first = pieces[d][:, :128]
        if d:
            first = first + pieces[d - 1][:, 384:]
        out += [first, pieces[d][:, 128:384]]
    out.append(pieces[3][:, 384:])
    return jnp.concatenate(out, axis=1)


def window(full, d):
    wide = full[:, 384 * d : 384 * d + 512]
    return pltpu.roll(wide, 512 - 32 * d, 1) if d else wide


def tn(a, b):
    return lax.dot_general(a, b, (((0,), (0,)), ((), ())), preferred_element_type=f32)


def nt(a, b):
    return lax.dot_general(a, b, (((1,), (1,)), ((), ())), preferred_element_type=f32)


def work(
    xg, win, wout, so, s_in, dxs, gwin, gwout, gsin, gsout,
    q_in, t_in, q_out, t_out, w_full, p_in, p_out,
):
    _, d, *_ = where_am_i()
    scale_in = s_in[:, pl.ds(pl.multiple_of(d * 256, 256), 256)]
    inv_in = 1.0 / scale_in
    for b in range(4):
        rows = slice(416 * b, 416 * b + 416)
        tangent = jnp.tanh(win[b].astype(f32) * inv_in)
        t_in[rows] = tangent
        q_in[rows] = (scale_in * tangent).astype(bf16)
    scale_out = spread(so, 1)
    inv_out = 1.0 / scale_out
    w_full[...] = spread(wout, 256)
    tangent = jnp.tanh(w_full[...] * inv_out)
    t_out[...] = tangent
    q_out[...] = (scale_out * tangent).astype(bf16)
    p_in[...] = jnp.zeros_like(p_in)
    p_out[...] = jnp.zeros_like(p_out)

    @pl.loop(0, 4)
    def _(j):
        low, high = xg[j, 0].astype(f32), xg[j, 1].astype(f32)

        def rows_of(k):
            pick = slice(8 * k, 8 * k + 8)
            left = low[:, pick].reshape(256, HALF)
            right = high[:, pick].reshape(256, HALF)
            return jnp.concatenate([left, right[:, : HALF - 128]], axis=1), right[:, HALF - 128 :]

        x, gate_tile = rows_of(0)
        g, _ = rows_of(1)
        x = x.astype(bf16)
        gate = gate_tile[:, 0:1]
        hidden = jnp.dot(x, q_in[...], preferred_element_type=f32)
        act, slope = gelu_parts(hidden)
        act = act.astype(bf16)
        back = nt(g.astype(bf16), q_out[...])
        gate_part = jnp.sum(act.astype(f32) * back, axis=1, keepdims=True)
        hidden_grad = (gate * back * slope).astype(bf16)
        out_grad = (gate * g).astype(bf16)
        p_in[...] += tn(x, hidden_grad)
        p_out[...] += tn(act, out_grad)
        dx = nt(hidden_grad, q_in[...])
        lane = lax.broadcasted_iota(jnp.int32, (256, 512), 1)
        top = gate_part.astype(bf16).astype(f32)
        rest = gate_part - top
        for k in range(4):
            piece = window(dx, k)
            piece = jnp.where(lane == 416, top, jnp.where(lane == 417, rest, piece))
            piece = piece.reshape(32, 8, 512)
            dxs[j, k % 2, k // 2] = jnp.concatenate(
                [piece[:, :, :256], piece[:, :, 256:]], axis=1
            ).astype(bf16)

    factor = 1024.0 ** -0.5
    total_s = jnp.zeros((1, 256), f32)
    for b in range(4):
        rows = slice(416 * b, 416 * b + 416)
        total = p_in[rows] * factor
        tangent = t_in[rows]
        sech = 1.0 - tangent * tangent
        gwin[b] = (total * sech).astype(bf16)
        scaled = win[b].astype(f32) * inv_in
        total_s += jnp.sum(total * (tangent - scaled * sech), axis=0, keepdims=True)
    gsin[...] = total_s
    total = p_out[...] * factor
    tangent = t_out[...]
    sech = 1.0 - tangent * tangent
    grad = total * sech
    sums = jnp.sum(total * (tangent - w_full[...] * inv_out * sech), axis=0, keepdims=True)
    for b in range(4):
        gwout[b] = window(grad, b)[:, :416].astype(bf16)
        gsout[b] = window(sums, b)


def send_out(
    dxs, gwin, gwout, gsin, gsout, picks,
    gt, gg, gw_in, gw_out, gs_in, gs_out,
    cbuf, sbuf, xbuf, rbuf, rb, obuf, tbuf, tsum,
    local_sem, c_send, c_recv, x_send, x_recv, w_send, w_recv, r_send, r_recv, t_send, t_recv,
):
    e, d, t, y, zl, zh, c = where_am_i()
    at, along, partner = neighbours()
    over, cross = at(0, 8), (e, d, 3 - t)
    greet(
        [at(dy, dz) for dz in range(16) for dy in range(4) if (dy, dz) != (0, 0)]
        + [along(dx) for dx in (1, 2, 3)]
        + [partner, cross]
    )
    c_copies = [
        remote(dxs.at[j, 1 - c], cbuf.at[j], c_send.at[j], c_recv.at[j], partner) for j in range(4)
    ]
    for j in (2, 1, 3, 0):
        c_copies[j].start()
    x_copies = []
    for j in (2, 1, 3):
        c_copies[j].wait_recv()
        for h in range(2):
            sbuf[j - 1, h] = (dxs[j, c, h].astype(f32) + cbuf[j, h].astype(f32)).astype(bf16)
        copy = remote(
            sbuf.at[j - 1], xbuf.at[j - 1], x_send.at[j - 1], x_recv.at[j - 1], along(4 - j)
        )
        copy.start()
        x_copies.append(copy)
    mine = pl.ds(pl.multiple_of(d * 256, 256), 256)
    w_copies = []
    for dx in (1, 3, 2):
        there = lax.rem(d + dx, 4)
        for k, (src, dst) in enumerate((
            (gsout.at[there], obuf.at[d]),
            (gsin, gs_in.at[d]),
            (gwin.at[there], gw_in.at[:, mine]),
            (gwout.at[there], gw_out.at[mine, :]),
        )):
            copy = remote(src, dst, w_send.at[k, dx - 1], w_recv.at[k, dx - 1], along(dx))
            copy.start()
            w_copies.append(copy)
    locals_ = [
        pltpu.make_async_copy(gsout.at[d], obuf.at[d], local_sem.at[0]),
        pltpu.make_async_copy(gsin, gs_in.at[d], local_sem.at[1]),
        pltpu.make_async_copy(gwin.at[d], gw_in.at[:, mine], local_sem.at[2]),
        pltpu.make_async_copy(gwout.at[d], gw_out.at[mine, :], local_sem.at[3]),
    ]
    for copy in locals_:
        copy.start()

    c_copies[0].wait_recv()
    for copy in x_copies:
        copy.wait_recv()
    for h in range(2):
        total = dxs[0, c, h].astype(f32) + cbuf[0, h].astype(f32)
        for k in range(3):
            total = total + xbuf[k, h].astype(f32)
        rbuf[32 * h : 32 * h + 32] = total.astype(bf16)
    own = pltpu.make_async_copy(rbuf.at[zh * 32], rb.at[zh, e], local_sem.at[4])
    own.start()
    for dz in (8, 7, 9, 6, 10, 5, 11, 4, 12, 3, 13, 2, 14, 1, 15, 0):
        for dy in range(4):
            if (dy, dz) == (0, 0):
                continue
            device = at(-dy, -dz)
            remote(
                rbuf.at[lax.div(device[2], 2) * 32 + (dz % 8) * 4 + dy], rb.at[zh, e],
                r_send, r_recv, device,
            ).start()

    locals_[0].wait()
    for copy in w_copies:
        copy.wait_recv()
    tsum[...] = obuf[0] + obuf[1] + obuf[2] + obuf[3]
    t_copies = []
    for k, device in enumerate((partner, over, cross)):
        copy = remote(tsum, tbuf.at[k], t_send.at[k], t_recv.at[k], device)
        copy.start()
        t_copies.append(copy)
    for copy in t_copies:
        copy.wait_recv()
    gs_out[...] = (tsum[...] + tbuf[0] + tbuf[1] + tbuf[2])[:, :416]

    own.wait()
    whole = rbuf.at[pl.ds(0, 63)]
    remote(whole, whole, r_send, r_recv, partner).wait()

    onehot = (lax.broadcasted_iota(jnp.int32, (256, 128), 1) == picks[...]).astype(bf16)
    left = jnp.zeros((128, 256), f32)
    right = jnp.zeros((128, 256), f32)
    gate = jnp.zeros((256, 128), f32)
    for h in range(2):
        got = rb[h].astype(f32)
        lo = got[:, :8].reshape(256, 256)
        hi = got[:, 8:].reshape(256, 256)
        left += tn(onehot, lo.astype(bf16))
        right += tn(onehot, hi.astype(bf16))
        gate += hi[:, 128:]
    gt[...] = jnp.concatenate([left, right[:, :160]], axis=1).astype(bf16)
    gg[...] = gate
    for copy in c_copies + x_copies + w_copies + t_copies:
        copy.wait_send()
    for copy in locals_[1:]:
        copy.wait()


DMA = pltpu.SemaphoreType.DMA


def struct(*shape, dtype=bf16):
    return jax.ShapeDtypeStruct(shape, dtype)


def local(tokens, grad_out, picks, gates, w_in, w_out, scale_in, scale_out):
    pick_col = picks.reshape(256, 1)
    gate_col = gates.reshape(256, 1).astype(f32)
    xg, win, wout, so = pl.pallas_call(
        bring_in,
        out_shape=(
            struct(4, 2, 32, 16, HALF),
            struct(4, 416, 256),
            struct(4, 256, 416),
            struct(4, 1, 416, dtype=f32),
        ),
        in_specs=[VMEM] * 4 + [ANY] * 2 + [VMEM],
        out_specs=(VMEM,) * 4,
        scratch_shapes=[
            pltpu.VMEM((32, 16, HALF), bf16),
            DMA((4,)),
            DMA((3, 3)), DMA((3, 3)),
            DMA((8,)), DMA((8,)),
            DMA((2, 8)), DMA((2, 8)),
            DMA((8,)), DMA((8,)),
            DMA((4, 8)), DMA((4, 8)),
        ],
        compiler_params=pltpu.CompilerParams(
            collective_id=0, has_side_effects=True, vmem_limit_bytes=40 * MIB
        ),
        name="bring_in",
    )(tokens, grad_out, pick_col, gate_col, w_in[0], w_out[0], scale_out)
    dxs, gwin, gwout, gsin, gsout = pl.pallas_call(
        work,
        out_shape=(
            struct(4, 2, 2, 32, 16, 256),
            struct(4, 416, 256),
            struct(4, 256, 416),
            struct(1, 256, dtype=f32),
            struct(4, 1, 512, dtype=f32),
        ),
        in_specs=[VMEM] * 5,
        out_specs=(VMEM,) * 5,
        scratch_shapes=[
            pltpu.VMEM((D, 256), bf16),
            pltpu.VMEM((D, 256), f32),
            pltpu.VMEM((256, D), bf16),
            pltpu.VMEM((256, D), f32),
            pltpu.VMEM((256, D), f32),
            pltpu.VMEM((D, 256), f32),
            pltpu.VMEM((256, D), f32),
        ],
        compiler_params=pltpu.CompilerParams(vmem_limit_bytes=56 * MIB),
        name="work",
    )(xg, win, wout, so, scale_in)
    gt, gg, gw_in, gw_out, gs_in, gs_out = pl.pallas_call(
        send_out,
        out_shape=(
            struct(128, 416),
            struct(256, 128, dtype=f32),
            struct(416, 1024),
            struct(1024, 416),
            struct(4, 1, 256, dtype=f32),
            struct(1, 416, dtype=f32),
        ),
        in_specs=[VMEM] * 6,
        out_specs=(VMEM, VMEM, ANY, ANY, VMEM, VMEM),
        scratch_shapes=[
            pltpu.VMEM((4, 2, 32, 16, 256), bf16),
            pltpu.VMEM((3, 2, 32, 16, 256), bf16),
            pltpu.VMEM((3, 2, 32, 16, 256), bf16),
            pltpu.VMEM((64, 16, 256), bf16),
            pltpu.VMEM((2, 32, 16, 256), bf16),
            pltpu.VMEM((4, 1, 512), f32),
            pltpu.VMEM((3, 1, 512), f32),
            pltpu.VMEM((1, 512), f32),
            DMA((5,)),
            DMA((4,)), DMA((4,)),
            DMA((3,)), DMA((3,)),
            DMA((4, 3)), DMA((4, 3)),
            DMA, DMA,
            DMA((3,)), DMA((3,)),
        ],
        compiler_params=pltpu.CompilerParams(
            collective_id=1, has_side_effects=True, vmem_limit_bytes=40 * MIB
        ),
        name="send_out",
    )(dxs, gwin, gwout, gsin, gsout, pick_col)
    gate_grad = (gg[:, 32] + gg[:, 33]).reshape(1, 32, 8)
    return gt, gate_grad, gw_in[None], gw_out[None], gs_in.reshape(1, 1024), gs_out


def solution(mesh):
    placed = (
        P(("expert", "dp"), None),
        P(("expert", "dp"), None),
        P(("expert", "dp"), None, None),
        P(("expert", "dp"), None, None),
        P("expert", "dp", "tensor"),
        P("expert", "tensor", "dp"),
        P("expert", "tensor"),
        P("expert", "dp"),
    )
    return jax.shard_map(
        local,
        mesh=mesh,
        in_specs=placed,
        out_specs=(
            P(("expert", "dp"), "tensor"),
            P(("expert", "dp"), None, None),
            P("expert", "dp", "tensor"),
            P("expert", "tensor", "dp"),
            P("expert", "tensor"),
            P("expert", "dp"),
        ),
        check_vma=False,
    )
```

```python
import functools

import jax
import jax.numpy as jnp
from jax import lax
from jax.experimental import pallas as pl
from jax.experimental.pallas import tpu as pltpu
from jax.sharding import PartitionSpec as P

gelu_coeff = 0.7978845608028654
cubic_coeff = 0.044715

D = 1664
HALF = 896
MIB = 1 << 20
f32, bf16 = jnp.float32, jnp.bfloat16
VMEM = pl.BlockSpec(memory_space=pltpu.VMEM)
ANY = pl.BlockSpec(memory_space=pl.ANY)
GROUPS = (0, 1, 7, 2, 6, 3, 5, 4)
FACTOR = 1024.0 ** -0.5


def where_am_i():
    e, d, t = lax.axis_index("expert"), lax.axis_index("dp"), lax.axis_index("tensor")
    y, zl = lax.div(e, 8), lax.rem(e, 8)
    zh, c = lax.div(t, 2), lax.rem(t, 2)
    return e, d, t, y, zl, zh, c


def neighbours():
    e, d, t, y, zl, zh, c = where_am_i()
    z = zh * 8 + zl

    def at(dy, dz):
        yy, zz = lax.rem(y + dy + 4, 4), lax.rem(z + dz + 16, 16)
        return (yy * 8 + lax.rem(zz, 8), d, lax.div(zz, 8) * 2 + c)

    def along(dx):
        return (e, lax.rem(d + dx, 4), t)

    return at, along, (e, d, t + 1 - 2 * c)


def greet(devices):
    barrier = pltpu.get_barrier_semaphore()
    for device in devices:
        pl.semaphore_signal(barrier, inc=1, device_id=device, device_id_type=pl.DeviceIdType.MESH)
    pl.semaphore_wait(barrier, len(devices))


def remote(src, dst, send, recv, device):
    return pltpu.make_async_remote_copy(
        src_ref=src, dst_ref=dst, send_sem=send, recv_sem=recv,
        device_id=device, device_id_type=pl.DeviceIdType.MESH,
    )


def gelu_parts(hidden):
    inner_arg = gelu_coeff * (hidden + cubic_coeff * hidden * hidden * hidden)
    tangent = jnp.tanh(inner_arg)
    output = 0.5 * hidden * (1.0 + tangent)
    gelu_slope = 0.5 * (1.0 + tangent) + 0.5 * hidden * (1.0 - tangent * tangent) * gelu_coeff * (
        1.0 + 3.0 * cubic_coeff * hidden * hidden
    )
    return output, gelu_slope


def window(full, d):
    wide = full[:, 384 * d : 384 * d + 512]
    return pltpu.roll(wide, 512 - 32 * d, 1) if d else wide


def tn(a, b):
    return lax.dot_general(a, b, (((0,), (0,)), ((), ())), preferred_element_type=f32)


def nt(a, b):
    return lax.dot_general(a, b, (((1,), (1,)), ((), ())), preferred_element_type=f32)


def kernel(
    tokens_hbm, grads_hbm, picks, gates, w_in, w_out, s_in, s_out,
    gt, gg, gw_in, gw_out, gs_in, gs_out,
    tokens, grads, onehot, stage, xg, win, wout, so,
    q_in, t_in, q_out, t_out, so_col, p_in, p_out,
    xs, ys, act, hid, gwin, gwout, gsin, gsout,
    dxs, cbuf, sbuf, xbuf, rbuf, rb, obuf, tbuf, tsum,
    local_sem, w_send, w_recv, a_send, a_recv, x_send, x_recv, f_send, f_recv, p_send, p_recv,
    c_send, c_recv, s_send, s_recv, g_send, g_recv, r_send, r_recv, t_send, t_recv,
):
    e, d, t, y, zl, zh, c = where_am_i()
    at, along, partner = neighbours()
    over, cross = at(0, 8), (e, d, 3 - t)
    mine = pl.ds(pl.multiple_of(d * 256, 256), 256)

    fetch = [
        pltpu.make_async_copy(tokens_hbm, tokens, local_sem.at[0]),
        pltpu.make_async_copy(grads_hbm, grads, local_sem.at[1]),
        pltpu.make_async_copy(w_in.at[:, mine], win.at[d], local_sem.at[2]),
        pltpu.make_async_copy(w_out.at[:, mine], wout.at[d], local_sem.at[3]),
        pltpu.make_async_copy(s_out, so.at[d], local_sem.at[4]),
    ]
    for copy in fetch:
        copy.start()
    greet(
        [at(dy, dz) for dz in range(16) for dy in range(4) if (dy, dz) != (0, 0)]
        + [along(dx) for dx in (1, 2, 3)]
        + [partner, cross]
    )

    w_copies = []
    for dx in (1, 3, 2):
        there = lax.rem(d + dx, 4)
        cols = pl.ds(pl.multiple_of(there * 256, 256), 256)
        for k, (src, dst) in enumerate(
            ((w_in.at[:, cols], win.at[d]), (w_out.at[:, cols], wout.at[d]), (s_out, so.at[d]))
        ):
            copy = remote(src, dst, w_send.at[k, dx - 1], w_recv.at[k, dx - 1], along(dx))
            copy.start()
            w_copies.append(copy)

    lane = lax.broadcasted_iota(jnp.int32, (8, 128), 1)
    gates32 = gates[...].astype(f32)
    onehot[...] = jnp.concatenate(
        [(lane == picks[:, k : k + 1]).astype(f32) for k in range(32)], axis=0
    ).astype(bf16)
    gate_tile = jnp.concatenate(
        [jnp.broadcast_to(gates32[:, k : k + 1], (8, 128)) for k in range(32)], axis=0
    )
    body = pl.ds(pl.multiple_of(c * HALF, 128), HALF - 128)

    def rows(ref):
        most = jnp.dot(onehot[...], ref[:, body], preferred_element_type=f32)
        last = jnp.dot(onehot[...], ref[:, HALF - 128 : HALF], preferred_element_type=f32)
        last = jnp.where(c == 0, last, gate_tile)
        return most.reshape(32, 8, HALF - 128), last.reshape(32, 8, 128)

    fetch[0].wait()
    fetch[1].wait()
    x_most, x_last = rows(tokens)
    g_most, g_last = rows(grads)
    stage[:, :, 0 : HALF - 128] = jnp.concatenate([x_most, g_most], axis=1).astype(bf16)
    stage[:, :, HALF - 128 : HALF] = jnp.concatenate([x_last, g_last], axis=1).astype(bf16)

    own = pltpu.make_async_copy(stage.at[e], xg.at[0, c, 0], local_sem.at[5])
    own.start()
    for dz in GROUPS:
        for dy in range(4):
            if (dy, dz) == (0, 0):
                continue
            way = dz if dz < 4 else dz - 8
            if dz == 4:
                way = 4 if dy < 2 else -4
            device = at(dy, way)
            remote(
                stage.at[device[0]], xg.at[0, c, dz * 4 + dy], a_send.at[dz], a_recv.at[dz], device
            ).start()

    def part(block, g):
        return xg.at[block, c, pl.ds(4 * g, 4)]

    def to_partner(block, g):
        return remote(part(block, g), part(block, g), p_send.at[block, g], p_recv.at[block, g], partner)

    def forth(g):
        return remote(part(0, g), part(1, g), x_send.at[0, g], x_recv.at[0, g], along(1))

    def back(g):
        return remote(part(0, g), part(3, g), x_send.at[1, g], x_recv.at[1, g], along(3))

    def onward(g):
        if GROUPS.index(g) % 2 == 0:
            return remote(part(1, g), part(2, g), f_send.at[g], f_recv.at[g], along(1))
        return remote(part(3, g), part(2, g), f_send.at[g], f_recv.at[g], along(3))

    def arrived(g):
        n = 3 if g == 0 else 4
        ref = xg.at[0, c, pl.ds(4 * g + 4 - n, n)]
        return remote(ref, ref, a_send.at[g], a_recv.at[g], partner)

    own.wait()
    for g in GROUPS:
        arrived(g).wait_recv()
        forth(g).start()
        back(g).start()
        to_partner(0, g).start()

    for copy in fetch[2:]:
        copy.wait()
    for copy in w_copies:
        copy.wait_recv()
    scale_in = s_in[:, mine]
    inv_in = 1.0 / scale_in
    for b in range(4):
        part_rows = slice(416 * b, 416 * b + 416)
        tangent = jnp.tanh(win[b].astype(f32) * inv_in)
        t_in[part_rows] = tangent
        q_in[part_rows] = (scale_in * tangent).astype(bf16)
        wide = jnp.concatenate([so[b], jnp.ones((1, 96), f32)], axis=1)
        col = jnp.broadcast_to(wide, (128, 512)).T[:416]
        so_col[part_rows] = col
        col = jnp.concatenate([col, col], axis=1)
        tangent = jnp.tanh(wout[b].astype(f32) * (1.0 / col))
        t_out[part_rows] = tangent
        q_out[part_rows] = (col * tangent).astype(bf16)

    c_copies = [
        remote(dxs.at[j, 1 - c], cbuf.at[j], c_send.at[j], c_recv.at[j], partner) for j in range(4)
    ]
    s_copies = [
        remote(sbuf.at[j - 1], xbuf.at[j - 1], s_send.at[j - 1], s_recv.at[j - 1], along(4 - j))
        for j in (1, 2, 3)
    ]

    def forward(j):
        for g in GROUPS:
            to_partner(j, g).wait_recv()
        low, high = xg[j, 0].astype(f32), xg[j, 1].astype(f32)

        def rows_of(k):
            pick = slice(8 * k, 8 * k + 8)
            left = low[:, pick].reshape(256, HALF)
            right = high[:, pick].reshape(256, HALF)
            return jnp.concatenate([left, right[:, : HALF - 128]], axis=1), right[:, HALF - 128 :]

        x, gate_rows = rows_of(0)
        g, _ = rows_of(1)
        x = x.astype(bf16)
        xs[j] = x
        gate = gate_rows[:, 0:1]
        ys[j] = (gate * g).astype(bf16)
        hidden = jnp.dot(x, q_in[...], preferred_element_type=f32)
        value, slope = gelu_parts(hidden)
        value = value.astype(bf16)
        act[j] = value
        back_prop = jnp.dot(g.astype(bf16), q_out[...], preferred_element_type=f32)
        gate_part = jnp.sum(value.astype(f32) * back_prop, axis=1, keepdims=True)
        hidden_grad = (gate * back_prop * slope).astype(bf16)
        hid[j] = hidden_grad
        dx = nt(hidden_grad, q_in[...])
        lanes = lax.broadcasted_iota(jnp.int32, (256, 512), 1)
        top = gate_part.astype(bf16).astype(f32)
        rest = gate_part - top
        for k in range(4):
            piece = window(dx, k)
            piece = jnp.where(lanes == 416, top, jnp.where(lanes == 417, rest, piece))
            piece = piece.reshape(32, 8, 512)
            dxs[j, k % 2, k // 2] = jnp.concatenate(
                [piece[:, :, :256], piece[:, :, 256:]], axis=1
            ).astype(bf16)
        c_copies[j].start()

    def weigh(j):
        into_in, into_out = tn(xs[j], hid[j]), tn(ys[j], act[j])
        if j:
            into_in, into_out = p_in[...] + into_in, p_out[...] + into_out
        p_in[...] = into_in
        p_out[...] = into_out

    def hand_over(j):
        c_copies[j].wait_recv()
        sbuf[j - 1] = (dxs[j, c].astype(f32) + cbuf[j].astype(f32)).astype(bf16)
        s_copies[j - 1].start()

    forward(0)
    weigh(0)
    for g in GROUPS:
        forth(g).wait_recv()
        back(g).wait_recv()
        onward(g).start()
        to_partner(1, g).start()
        to_partner(3, g).start()
    forward(1)
    weigh(1)
    hand_over(1)
    forward(3)
    for g in GROUPS:
        onward(g).wait_recv()
        to_partner(2, g).start()
    hand_over(3)
    weigh(3)
    forward(2)
    weigh(2)
    hand_over(2)

    total_s = jnp.zeros((1, 256), f32)
    for b in range(4):
        part_rows = slice(416 * b, 416 * b + 416)
        total = p_in[part_rows] * FACTOR
        tangent = t_in[part_rows]
        sech = 1.0 - tangent * tangent
        gwin[b] = (total * sech).astype(bf16)
        scaled = win[b].astype(f32) * inv_in
        total_s += jnp.sum(total * (tangent - scaled * sech), axis=0, keepdims=True)
        total = p_out[part_rows] * FACTOR
        tangent = t_out[part_rows]
        sech = 1.0 - tangent * tangent
        gwout[b] = (total * sech).astype(bf16)
        inv = 1.0 / so_col[part_rows]
        scaled = wout[b].astype(f32) * jnp.concatenate([inv, inv], axis=1)
        terms = total * (tangent - scaled * sech)
        terms = terms[:, :128] + terms[:, 128:]
        terms = jnp.concatenate([terms, jnp.zeros((96, 128), f32)], axis=0)
        gsout[b] = jnp.sum(terms.T, axis=0, keepdims=True)
    gsin[...] = total_s

    c_copies[0].wait_recv()
    total = dxs[0, c].astype(f32) + cbuf[0].astype(f32)
    for copy in s_copies:
        copy.wait_recv()
    for k in range(3):
        total = total + xbuf[k].astype(f32)
    rbuf[...] = total.astype(bf16).reshape(64, 16, 256)
    keep = pltpu.make_async_copy(rbuf.at[zh * 32], rb.at[zh, e], local_sem.at[6])
    keep.start()
    for dz in (8, 7, 9, 6, 10, 5, 11, 4, 12, 3, 13, 2, 14, 1, 15, 0):
        for dy in range(4):
            if (dy, dz) == (0, 0):
                continue
            device = at(-dy, -dz)
            remote(
                rbuf.at[lax.div(device[2], 2) * 32 + (dz % 8) * 4 + dy], rb.at[zh, e],
                r_send, r_recv, device,
            ).start()

    g_copies = []
    for k, (src, dst) in enumerate((
        (gsout, obuf.at[d]),
        (gsin, gs_in.at[d]),
        (gwin, gw_in.at[:, mine]),
        (gwout, gw_out.at[:, mine]),
    )):
        for dx in (1, 3, 2):
            block = src if k == 1 else src.at[lax.rem(d + dx, 4)]
            copy = remote(block, dst, g_send.at[k, dx - 1], g_recv.at[k, dx - 1], along(dx))
            copy.start()
            g_copies.append(copy)
    stay = [
        pltpu.make_async_copy(gsout.at[d], obuf.at[d], local_sem.at[7]),
        pltpu.make_async_copy(gsin, gs_in.at[d], local_sem.at[8]),
        pltpu.make_async_copy(gwin.at[d], gw_in.at[:, mine], local_sem.at[9]),
        pltpu.make_async_copy(gwout.at[d], gw_out.at[:, mine], local_sem.at[10]),
    ]
    for copy in stay:
        copy.start()

    stay[0].wait()
    for copy in g_copies[:3]:
        copy.wait_recv()
    tsum[...] = obuf[0] + obuf[1] + obuf[2] + obuf[3]
    t_copies = []
    for k, device in enumerate((partner, over, cross)):
        copy = remote(tsum, tbuf.at[k], t_send.at[k], t_recv.at[k], device)
        copy.start()
        t_copies.append(copy)
    for copy in t_copies:
        copy.wait_recv()
    gs_out[...] = (tsum[...] + tbuf[0] + tbuf[1] + tbuf[2])[:, :416]

    keep.wait()
    returned = rbuf.at[pl.ds(0, 63)]
    remote(returned, returned, r_send, r_recv, partner).wait()
    left = jnp.zeros((256, 128), f32)
    right = jnp.zeros((256, 128), f32)
    gate = jnp.zeros((256, 128), f32)
    for h in range(2):
        got = rb[h].astype(f32)
        lo = got[:, :8].reshape(256, 256)
        hi = got[:, 8:].reshape(256, 256)
        left += tn(lo.astype(bf16), onehot[...])
        right += tn(hi.astype(bf16), onehot[...])
        gate += hi[:, 128:]
    gt[0:256] = left.astype(bf16)
    gt[256:416] = right[:160].astype(bf16)
    gates_out = jnp.zeros((8, 128), f32)
    for k in range(32):
        rows8 = gate[8 * k : 8 * k + 8]
        gates_out = jnp.where(lane == k, rows8[:, 32:33] + rows8[:, 33:34], gates_out)
    gg[...] = gates_out[:, :32]

    for g in GROUPS:
        arrived(g).wait_send()
        forth(g).wait_send()
        back(g).wait_send()
        onward(g).wait_send()
        for block in range(4):
            to_partner(block, g).wait_send()
    for copy in w_copies + c_copies + s_copies + t_copies + g_copies:
        copy.wait_send()
    for copy in g_copies[3:]:
        copy.wait_recv()
    for copy in stay[1:]:
        copy.wait()


DMA = pltpu.SemaphoreType.DMA


def struct(*shape, dtype=bf16):
    return jax.ShapeDtypeStruct(shape, dtype)


def local(tokens, grad_out, picks, gates, w_in, w_out, scale_in, scale_out):
    gt, gg, gw_in, gw_out, gs_in, gs_out = pl.pallas_call(
        kernel,
        out_shape=(
            struct(416, 128),
            struct(8, 32, dtype=f32),
            struct(416, 1024),
            struct(416, 1024),
            struct(4, 1, 256, dtype=f32),
            struct(1, 416, dtype=f32),
        ),
        in_specs=[ANY, ANY, VMEM, VMEM, ANY, ANY, VMEM, VMEM],
        out_specs=(VMEM, VMEM, ANY, ANY, VMEM, VMEM),
        scratch_shapes=[
            pltpu.VMEM((128, D), bf16),
            pltpu.VMEM((128, D), bf16),
            pltpu.VMEM((256, 128), bf16),
            pltpu.VMEM((32, 16, HALF), bf16),
            pltpu.VMEM((4, 2, 32, 16, HALF), bf16),
            pltpu.VMEM((4, 416, 256), bf16),
            pltpu.VMEM((4, 416, 256), bf16),
            pltpu.VMEM((4, 1, 416), f32),
            pltpu.VMEM((D, 256), bf16),
            pltpu.VMEM((D, 256), f32),
            pltpu.VMEM((D, 256), bf16),
            pltpu.VMEM((D, 256), f32),
            pltpu.VMEM((D, 128), f32),
            pltpu.VMEM((D, 256), f32),
            pltpu.VMEM((D, 256), f32),
            pltpu.VMEM((4, 256, D), bf16),
            pltpu.VMEM((4, 256, D), bf16),
            pltpu.VMEM((4, 256, 256), bf16),
            pltpu.VMEM((4, 256, 256), bf16),
            pltpu.VMEM((4, 416, 256), bf16),
            pltpu.VMEM((4, 416, 256), bf16),
            pltpu.VMEM((1, 256), f32),
            pltpu.VMEM((4, 1, 512), f32),
            pltpu.VMEM((4, 2, 2, 32, 16, 256), bf16),
            pltpu.VMEM((4, 2, 32, 16, 256), bf16),
            pltpu.VMEM((3, 2, 32, 16, 256), bf16),
            pltpu.VMEM((3, 2, 32, 16, 256), bf16),
            pltpu.VMEM((64, 16, 256), bf16),
            pltpu.VMEM((2, 32, 16, 256), bf16),
            pltpu.VMEM((4, 1, 512), f32),
            pltpu.VMEM((3, 1, 512), f32),
            pltpu.VMEM((1, 512), f32),
            DMA((11,)),
            DMA((3, 3)), DMA((3, 3)),
            DMA((8,)), DMA((8,)),
            DMA((2, 8)), DMA((2, 8)),
            DMA((8,)), DMA((8,)),
            DMA((4, 8)), DMA((4, 8)),
            DMA((4,)), DMA((4,)),
            DMA((3,)), DMA((3,)),
            DMA((4, 3)), DMA((4, 3)),
            DMA, DMA,
            DMA((3,)), DMA((3,)),
        ],
        compiler_params=pltpu.CompilerParams(
            collective_id=0, has_side_effects=True, vmem_limit_bytes=58 * MIB
        ),
        name="moe_backward",
    )(
        tokens, grad_out, picks[0].T, gates[0].T, w_in[0], w_out[0].T, scale_in, scale_out,
    )
    return gt.T, gg.T[None], gw_in[None], gw_out.T[None], gs_in.reshape(1, 1024), gs_out


def solution(mesh):
    placed = (
        P(("expert", "dp"), None),
        P(("expert", "dp"), None),
        P(("expert", "dp"), None, None),
        P(("expert", "dp"), None, None),
        P("expert", "dp", "tensor"),
        P("expert", "tensor", "dp"),
        P("expert", "tensor"),
        P("expert", "dp"),
    )
    return jax.shard_map(
        local,
        mesh=mesh,
        in_specs=placed,
        out_specs=(
            P(("expert", "dp"), "tensor"),
            P(("expert", "dp"), None, None),
            P("expert", "dp", "tensor"),
            P("expert", "tensor", "dp"),
            P("expert", "tensor"),
            P("expert", "dp"),
        ),
        check_vma=False,
    )
```

```python
import functools

import jax
import jax.numpy as jnp
from jax import lax
from jax.experimental import pallas as pl
from jax.experimental.pallas import tpu as pltpu
from jax.sharding import PartitionSpec as P

gelu_coeff = 0.7978845608028654
cubic_coeff = 0.044715

D = 1664
HALF = 896
MIB = 1 << 20
f32, bf16 = jnp.float32, jnp.bfloat16
VMEM = pl.BlockSpec(memory_space=pltpu.VMEM)
ANY = pl.BlockSpec(memory_space=pl.ANY)
GROUPS = (0, 1, 7, 2, 6, 3, 5, 4)
FACTOR = 1024.0 ** -0.5


def where_am_i():
    e, d, t = lax.axis_index("expert"), lax.axis_index("dp"), lax.axis_index("tensor")
    y, zl = lax.div(e, 8), lax.rem(e, 8)
    zh, c = lax.div(t, 2), lax.rem(t, 2)
    return e, d, t, y, zl, zh, c


def neighbours():
    e, d, t, y, zl, zh, c = where_am_i()
    z = zh * 8 + zl

    def at(dy, dz):
        yy, zz = lax.rem(y + dy + 4, 4), lax.rem(z + dz + 16, 16)
        return (yy * 8 + lax.rem(zz, 8), d, lax.div(zz, 8) * 2 + c)

    def along(dx):
        return (e, lax.rem(d + dx, 4), t)

    return at, along, (e, d, t + 1 - 2 * c)


def greet(devices):
    barrier = pltpu.get_barrier_semaphore()
    for device in devices:
        pl.semaphore_signal(barrier, inc=1, device_id=device, device_id_type=pl.DeviceIdType.MESH)
    return lambda: pl.semaphore_wait(barrier, len(devices))


def remote(src, dst, send, recv, device):
    return pltpu.make_async_remote_copy(
        src_ref=src, dst_ref=dst, send_sem=send, recv_sem=recv,
        device_id=device, device_id_type=pl.DeviceIdType.MESH,
    )


def gelu_parts(hidden):
    inner_arg = gelu_coeff * (hidden + cubic_coeff * hidden * hidden * hidden)
    tangent = jnp.tanh(inner_arg)
    output = 0.5 * hidden * (1.0 + tangent)
    gelu_slope = 0.5 * (1.0 + tangent) + 0.5 * hidden * (1.0 - tangent * tangent) * gelu_coeff * (
        1.0 + 3.0 * cubic_coeff * hidden * hidden
    )
    return output, gelu_slope


def window(full, d):
    wide = full[:, 384 * d : 384 * d + 512]
    return pltpu.roll(wide, 512 - 32 * d, 1) if d else wide


def tn(a, b):
    return lax.dot_general(a, b, (((0,), (0,)), ((), ())), preferred_element_type=f32)


def nt(a, b):
    return lax.dot_general(a, b, (((1,), (1,)), ((), ())), preferred_element_type=f32)


def kernel(
    tokens_hbm, grads_hbm, picks, gates, w_in, w_out, s_in, s_out,
    gt, gg, gw_in, gw_out, gs_in, gs_out,
    tokens, grads, onehot, stage, xg, win, wout, so,
    q_in, t_in, q_out, t_out, so_col, p_in, p_out,
    xs, ys, act, hid, gwin, gwout, gsin, gsout,
    dxs, dxg, cbuf, cgate, sbuf, sgate, vbuf, xbuf, xgate, pair, rbuf, rb, stand, obuf, tbuf, tsum,
    local_sem, w_send, w_recv, a_send, a_recv, x_send, x_recv, f_send, f_recv, p_send, p_recv,
    c_send, c_recv, s_send, s_recv, g_send, g_recv, r_send, r_recv, t_send, t_recv,
):
    e, d, t, y, zl, zh, c = where_am_i()
    at, along, partner = neighbours()
    over, cross = at(0, 8), (e, d, 3 - t)
    mine = pl.ds(pl.multiple_of(d * 256, 256), 256)

    fetch = [
        pltpu.make_async_copy(tokens_hbm, tokens, local_sem.at[0]),
        pltpu.make_async_copy(grads_hbm, grads, local_sem.at[1]),
        pltpu.make_async_copy(w_in.at[:, mine], win.at[d], local_sem.at[2]),
        pltpu.make_async_copy(w_out.at[:, mine], wout.at[d], local_sem.at[3]),
        pltpu.make_async_copy(s_out, so.at[d], local_sem.at[4]),
    ]
    for copy in fetch:
        copy.start()
    all_in = greet(
        [along(dx) for dx in (1, 2, 3)]
        + [partner, cross]
        + [at(dy, dz) for dz in range(16) for dy in range(4) if (dy, dz) != (0, 0)]
    )

    lane = lax.broadcasted_iota(jnp.int32, (8, 128), 1)
    gates32 = gates[...].astype(f32)
    onehot[...] = jnp.concatenate(
        [(lane == picks[:, k : k + 1]).astype(f32) for k in range(32)], axis=0
    ).astype(bf16)
    gate_tile = jnp.concatenate(
        [jnp.broadcast_to(gates32[:, k : k + 1], (8, 128)) for k in range(32)], axis=0
    )
    body = pl.ds(pl.multiple_of(c * HALF, 128), HALF - 128)

    def rows(ref):
        most = jnp.dot(onehot[...], ref[:, body], preferred_element_type=f32)
        last = jnp.dot(onehot[...], ref[:, HALF - 128 : HALF], preferred_element_type=f32)
        last = jnp.where(c == 0, last, gate_tile)
        return most.reshape(32, 8, HALF - 128), last.reshape(32, 8, 128)

    fetch[0].wait()
    fetch[1].wait()
    x_most, x_last = rows(tokens)
    g_most, g_last = rows(grads)
    stage[:, :, 0 : HALF - 128] = jnp.concatenate([x_most, g_most], axis=1).astype(bf16)
    stage[:, :, HALF - 128 : HALF] = jnp.concatenate([x_last, g_last], axis=1).astype(bf16)

    all_in()

    w_copies = []
    for dx in (1, 3, 2):
        there = lax.rem(d + dx, 4)
        cols = pl.ds(pl.multiple_of(there * 256, 256), 256)
        for k, (src, dst) in enumerate(
            ((w_in.at[:, cols], win.at[d]), (w_out.at[:, cols], wout.at[d]), (s_out, so.at[d]))
        ):
            copy = remote(src, dst, w_send.at[k, dx - 1], w_recv.at[k, dx - 1], along(dx))
            copy.start()
            w_copies.append(copy)

    own = pltpu.make_async_copy(stage.at[e], xg.at[0, c, 0], local_sem.at[5])
    own.start()
    for dz in GROUPS:
        for dy in range(4):
            if (dy, dz) == (0, 0):
                continue
            way = dz if dz < 4 else dz - 8
            if dz == 4:
                way = 4 if dy < 2 else -4
            device = at(dy, way)
            remote(
                stage.at[device[0]], xg.at[0, c, dz * 4 + dy], a_send.at[dz], a_recv.at[dz], device
            ).start()

    def part(block, g):
        return xg.at[block, c, pl.ds(4 * g, 4)]

    def to_partner(block, g):
        return remote(part(block, g), part(block, g), p_send.at[block, g], p_recv.at[block, g], partner)

    def forth(g):
        return remote(part(0, g), part(1, g), x_send.at[0, g], x_recv.at[0, g], along(1))

    def back(g):
        return remote(part(0, g), part(3, g), x_send.at[1, g], x_recv.at[1, g], along(3))

    def onward(g):
        if GROUPS.index(g) % 2 == 0:
            return remote(part(1, g), part(2, g), f_send.at[g], f_recv.at[g], along(1))
        return remote(part(3, g), part(2, g), f_send.at[g], f_recv.at[g], along(3))

    def arrived(g):
        n = 3 if g == 0 else 4
        ref = xg.at[0, c, pl.ds(4 * g + 4 - n, n)]
        return remote(ref, ref, a_send.at[g], a_recv.at[g], partner)

    own.wait()
    for g in GROUPS:
        arrived(g).wait_recv()
        forth(g).start()
        back(g).start()
        to_partner(0, g).start()

    for copy in fetch[2:]:
        copy.wait()
    for copy in w_copies:
        copy.wait_recv()
    scale_in = s_in[:, mine]
    inv_in = 1.0 / scale_in
    for b in range(4):
        part_rows = slice(416 * b, 416 * b + 416)
        tangent = jnp.tanh(win[b].astype(f32) * inv_in)
        t_in[part_rows] = tangent
        q_in[part_rows] = (scale_in * tangent).astype(bf16)
        wide = jnp.concatenate([so[b], jnp.ones((1, 96), f32)], axis=1)
        col = jnp.broadcast_to(wide, (128, 512)).T[:416]
        so_col[part_rows] = col
        col = jnp.concatenate([col, col], axis=1)
        tangent = jnp.tanh(wout[b].astype(f32) * (1.0 / col))
        t_out[part_rows] = tangent
        q_out[part_rows] = (col * tangent).astype(bf16)

    c_copies = [
        (
            remote(dxs.at[j, 1 - c], cbuf.at[j], c_send.at[0, j], c_recv.at[0, j], partner),
            remote(dxg.at[j], cgate.at[j], c_send.at[1, j], c_recv.at[1, j], partner),
        )
        for j in range(4)
    ]
    gate_copies = [
        remote(sgate.at[j - 1], xgate.at[j - 1], s_send.at[j - 1], s_recv.at[j - 1], along(4 - j))
        for j in (1, 2, 3)
    ]
    ahead = [along(1), along(3)]
    half = [pl.ds(0, 64), pl.ds(64, 64)]
    via = [
        remote(sbuf.at[1, half[k]], vbuf.at[k], s_send.at[3 + k], s_recv.at[3 + k], ahead[k])
        for k in range(2)
    ]
    alone = [
        remote(sbuf.at[2 - 2 * k, half[1 - k]], xbuf.at[k, half[1 - k]], s_send.at[5 + k], s_recv.at[5 + k], ahead[k])
        for k in range(2)
    ]
    joint = [
        remote(sbuf.at[2 - 2 * k, half[k]], xbuf.at[k, half[k]], s_send.at[7 + k], s_recv.at[7 + k], ahead[k])
        for k in range(2)
    ]

    def forward(j):
        for g in GROUPS:
            to_partner(j, g).wait_recv()
        low, high = xg[j, 0].astype(f32), xg[j, 1].astype(f32)

        def rows_of(k):
            pick = slice(8 * k, 8 * k + 8)
            left = low[:, pick].reshape(256, HALF)
            right = high[:, pick].reshape(256, HALF)
            return jnp.concatenate([left, right[:, : HALF - 128]], axis=1), right[:, HALF - 128 :]

        x, gate_rows = rows_of(0)
        g, _ = rows_of(1)
        x = x.astype(bf16)
        xs[j] = x
        gate = gate_rows[:, 0:1]
        ys[j] = (gate * g).astype(bf16)
        hidden = jnp.dot(x, q_in[...], preferred_element_type=f32)
        value, slope = gelu_parts(hidden)
        value = value.astype(bf16)
        act[j] = value
        back_prop = jnp.dot(g.astype(bf16), q_out[...], preferred_element_type=f32)
        gate_part = jnp.sum(value.astype(f32) * back_prop, axis=1, keepdims=True)
        hidden_grad = (gate * back_prop * slope).astype(bf16)
        hid[j] = hidden_grad
        dx = nt(hidden_grad, q_in[...])
        dxs[j] = dx.astype(bf16).reshape(2, 128, D)
        compact = jnp.zeros((8, 128), f32)
        for k in range(32):
            compact = jnp.where(lane == k, gate_part[8 * k : 8 * k + 8], compact)
        dxg[j] = compact
        for copy in c_copies[j]:
            copy.start()

    def weigh(j):
        into_in, into_out = tn(xs[j], hid[j]), tn(ys[j], act[j])
        if j:
            into_in, into_out = p_in[...] + into_in, p_out[...] + into_out
        p_in[...] = into_in
        p_out[...] = into_out

    def hand_over(j):
        for copy in c_copies[j]:
            copy.wait_recv()
        sbuf[j - 1] = (dxs[j, c].astype(f32) + cbuf[j].astype(f32)).astype(bf16)
        sgate[j - 1] = dxg[j] + cgate[j]
        gate_copies[j - 1].start()
        if j == 2:
            for copy in via:
                copy.start()
        else:
            alone[0 if j == 3 else 1].start()

    forward(0)
    weigh(0)
    for g in GROUPS:
        forth(g).wait_recv()
        back(g).wait_recv()
        onward(g).start()
        to_partner(1, g).start()
        to_partner(3, g).start()
    forward(1)
    weigh(1)
    hand_over(1)
    forward(3)
    for g in GROUPS:
        onward(g).wait_recv()
        to_partner(2, g).start()
    hand_over(3)
    weigh(3)
    forward(2)
    weigh(2)
    hand_over(2)

    for k in range(2):
        via[k].wait_recv()
        rows64 = slice(64 * k, 64 * k + 64)
        sbuf[2 - 2 * k, rows64] = (
            sbuf[2 - 2 * k, rows64].astype(f32) + vbuf[k].astype(f32)
        ).astype(bf16)
        joint[k].start()
    total_s = jnp.zeros((1, 256), f32)
    for b in range(4):
        part_rows = slice(416 * b, 416 * b + 416)
        total = p_in[part_rows] * FACTOR
        tangent = t_in[part_rows]
        sech = 1.0 - tangent * tangent
        gwin[b] = (total * sech).astype(bf16)
        scaled = win[b].astype(f32) * inv_in
        total_s += jnp.sum(total * (tangent - scaled * sech), axis=0, keepdims=True)
        total = p_out[part_rows] * FACTOR
        tangent = t_out[part_rows]
        sech = 1.0 - tangent * tangent
        gwout[b] = (total * sech).astype(bf16)
        inv = 1.0 / so_col[part_rows]
        scaled = wout[b].astype(f32) * jnp.concatenate([inv, inv], axis=1)
        terms = total * (tangent - scaled * sech)
        terms = terms[:, :128] + terms[:, 128:]
        terms = jnp.concatenate([terms, jnp.zeros((96, 128), f32)], axis=0)
        gsout[b] = jnp.sum(terms.T, axis=0, keepdims=True)
    gsin[...] = total_s

    for copy in c_copies[0]:
        copy.wait_recv()
    for copy in gate_copies + alone + joint:
        copy.wait_recv()
    total = (
        dxs[0, c].astype(f32) + cbuf[0].astype(f32) + xbuf[0].astype(f32) + xbuf[1].astype(f32)
    )
    gates_sum = dxg[0] + cgate[0] + xgate[0] + xgate[1] + xgate[2]
    gates_sum = jnp.where(c == 0, gates_sum, pltpu.roll(gates_sum, 112, 1))
    gate_col = jnp.concatenate(
        [jnp.broadcast_to(gates_sum[:, k : k + 1], (8, 128)) for k in range(16)], axis=0
    )
    top = gate_col.astype(bf16).astype(f32)
    rest = gate_col - top
    first = lax.broadcasted_iota(jnp.int32, (128, 128), 1)
    extra = jnp.where(first == 32, top, rest)
    own_half = pl.ds(pl.multiple_of(c * 16, 16), 16)
    for k in range(4):
        piece = window(total, k)
        last = jnp.where((first == 32) | (first == 33), extra, piece[:, 384:])
        piece = jnp.concatenate([piece[:, :384], last], axis=1).reshape(16, 8, 512)
        piece = jnp.concatenate([piece[:, :, :256], piece[:, :, 256:]], axis=1).astype(bf16)
        pair[k % 2, k // 2] = piece
    swap = remote(
        pair.at[1 - c], rbuf.at[:, own_half], r_send.at[1], r_recv.at[1], partner
    )
    swap.start()
    rbuf[:, own_half] = pair[c]
    swap.wait_recv()
    keep = pltpu.make_async_copy(rbuf.at[zh, 0], rb.at[zh, e], local_sem.at[6])
    keep.start()
    for dz in (8, 7, 9, 6, 10, 5, 11, 4, 12, 3, 13, 2, 14, 1, 15, 0):
        for dy in range(4):
            if (dy, dz) == (0, 0):
                continue
            device = at(-dy, -dz)
            remote(
                rbuf.at[lax.div(device[2], 2), (dz % 8) * 4 + dy], rb.at[zh, e],
                r_send.at[0], r_recv.at[0], device,
            ).start()

    g_copies = []
    for k, (src, dst) in enumerate((
        (gsout, obuf.at[d]),
        (gsin, gs_in.at[d]),
        (gwin, gw_in.at[:, mine]),
        (gwout, gw_out.at[:, mine]),
    )):
        for dx in (1, 3, 2):
            block = src if k == 1 else src.at[lax.rem(d + dx, 4)]
            copy = remote(block, dst, g_send.at[k, dx - 1], g_recv.at[k, dx - 1], along(dx))
            copy.start()
            g_copies.append(copy)
    stay = [
        pltpu.make_async_copy(gsout.at[d], obuf.at[d], local_sem.at[7]),
        pltpu.make_async_copy(gsin, gs_in.at[d], local_sem.at[8]),
        pltpu.make_async_copy(gwin.at[d], gw_in.at[:, mine], local_sem.at[9]),
        pltpu.make_async_copy(gwout.at[d], gw_out.at[:, mine], local_sem.at[10]),
    ]
    for copy in stay:
        copy.start()

    stay[0].wait()
    for copy in g_copies[:3]:
        copy.wait_recv()
    tsum[...] = obuf[0] + obuf[1] + obuf[2] + obuf[3]
    t_copies = []
    for k, device in enumerate((partner, over, cross)):
        copy = remote(tsum, tbuf.at[k], t_send.at[k], t_recv.at[k], device)
        copy.start()
        t_copies.append(copy)
    for copy in t_copies:
        copy.wait_recv()
    gs_out[...] = (tsum[...] + tbuf[0] + tbuf[1] + tbuf[2])[:, :416]

    keep.wait()
    returned = stand.at[pl.ds(0, 63)]
    remote(returned, returned, r_send.at[0], r_recv.at[0], partner).wait()
    left = jnp.zeros((256, 128), f32)
    right = jnp.zeros((256, 128), f32)
    gate = jnp.zeros((256, 128), f32)
    for h in range(2):
        got = rb[h].astype(f32)
        lo = got[:, :8].reshape(256, 256)
        hi = got[:, 8:].reshape(256, 256)
        left += tn(lo.astype(bf16), onehot[...])
        right += tn(hi.astype(bf16), onehot[...])
        gate += hi[:, 128:]
    gt[0:256] = left.astype(bf16)
    gt[256:416] = right[:160].astype(bf16)
    gates_out = jnp.zeros((8, 128), f32)
    for k in range(32):
        rows8 = gate[8 * k : 8 * k + 8]
        gates_out = jnp.where(lane == k, rows8[:, 32:33] + rows8[:, 33:34], gates_out)
    gg[...] = gates_out[:, :32]

    for g in GROUPS:
        arrived(g).wait_send()
        forth(g).wait_send()
        back(g).wait_send()
        onward(g).wait_send()
        for block in range(4):
            to_partner(block, g).wait_send()
    for copy in w_copies + via + alone + joint + gate_copies + t_copies + g_copies + [swap]:
        copy.wait_send()
    for pair_of in c_copies:
        for copy in pair_of:
            copy.wait_send()
    for copy in g_copies[3:]:
        copy.wait_recv()
    for copy in stay[1:]:
        copy.wait()


DMA = pltpu.SemaphoreType.DMA


def struct(*shape, dtype=bf16):
    return jax.ShapeDtypeStruct(shape, dtype)


def settle(*refs):
    ins, outs, sems = refs[:6], refs[6:12], refs[12]
    copies = [pltpu.make_async_copy(ins[k], outs[k], sems.at[k]) for k in range(6)]
    for copy in copies:
        copy.start()
    for copy in copies:
        copy.wait()


def local(tokens, grad_out, picks, gates, w_in, w_out, scale_in, scale_out):
    shapes = (
        struct(416, 128),
        struct(8, 32, dtype=f32),
        struct(416, 1024),
        struct(416, 1024),
        struct(4, 1, 256, dtype=f32),
        struct(1, 416, dtype=f32),
    )
    results = pl.pallas_call(
        kernel,
        out_shape=shapes,
        in_specs=[ANY, ANY, VMEM, VMEM, ANY, ANY, VMEM, VMEM],
        out_specs=(VMEM, VMEM, ANY, ANY, VMEM, VMEM),
        scratch_shapes=[
            pltpu.VMEM((128, D), bf16),
            pltpu.VMEM((128, D), bf16),
            pltpu.VMEM((256, 128), bf16),
            pltpu.VMEM((32, 16, HALF), bf16),
            pltpu.VMEM((4, 2, 32, 16, HALF), bf16),
            pltpu.VMEM((4, 416, 256), bf16),
            pltpu.VMEM((4, 416, 256), bf16),
            pltpu.VMEM((4, 1, 416), f32),
            pltpu.VMEM((D, 256), bf16),
            pltpu.VMEM((D, 256), f32),
            pltpu.VMEM((D, 256), bf16),
            pltpu.VMEM((D, 256), f32),
            pltpu.VMEM((D, 128), f32),
            pltpu.VMEM((D, 256), f32),
            pltpu.VMEM((D, 256), f32),
            pltpu.VMEM((4, 256, D), bf16),
            pltpu.VMEM((4, 256, D), bf16),
            pltpu.VMEM((4, 256, 256), bf16),
            pltpu.VMEM((4, 256, 256), bf16),
            pltpu.VMEM((4, 416, 256), bf16),
            pltpu.VMEM((4, 416, 256), bf16),
            pltpu.VMEM((1, 256), f32),
            pltpu.VMEM((4, 1, 512), f32),
            pltpu.VMEM((4, 2, 128, D), bf16),
            pltpu.VMEM((4, 8, 128), f32),
            pltpu.VMEM((4, 128, D), bf16),
            pltpu.VMEM((4, 8, 128), f32),
            pltpu.VMEM((3, 128, D), bf16),
            pltpu.VMEM((3, 8, 128), f32),
            pltpu.VMEM((2, 64, D), bf16),
            pltpu.VMEM((2, 128, D), bf16),
            pltpu.VMEM((3, 8, 128), f32),
            pltpu.VMEM((2, 2, 16, 16, 256), bf16),
            pltpu.VMEM((2, 32, 16, 256), bf16),
            pltpu.VMEM((2, 32, 16, 256), bf16),
            pltpu.VMEM((64, 16, 256), bf16),
            pltpu.VMEM((4, 1, 512), f32),
            pltpu.VMEM((3, 1, 512), f32),
            pltpu.VMEM((1, 512), f32),
            DMA((11,)),
            DMA((3, 3)), DMA((3, 3)),
            DMA((8,)), DMA((8,)),
            DMA((2, 8)), DMA((2, 8)),
            DMA((8,)), DMA((8,)),
            DMA((4, 8)), DMA((4, 8)),
            DMA((2, 4)), DMA((2, 4)),
            DMA((9,)), DMA((9,)),
            DMA((4, 3)), DMA((4, 3)),
            DMA((2,)), DMA((2,)),
            DMA((3,)), DMA((3,)),
        ],
        compiler_params=pltpu.CompilerParams(
            collective_id=0, has_side_effects=True, vmem_limit_bytes=58 * MIB
        ),
        name="moe_backward",
    )(
        tokens, grad_out, picks[0].T, gates[0].T, w_in[0], w_out[0].T, scale_in, scale_out,
    )
    gt, gg, gw_in, gw_out, gs_in, gs_out = pl.pallas_call(
        settle,
        out_shape=shapes,
        in_specs=[ANY] * 6,
        out_specs=(ANY,) * 6,
        scratch_shapes=[DMA((6,))],
        name="settle",
    )(*results)
    return gt.T, gg.T[None], gw_in[None], gw_out.T[None], gs_in.reshape(1, 1024), gs_out


def solution(mesh):
    placed = (
        P(("expert", "dp"), None),
        P(("expert", "dp"), None),
        P(("expert", "dp"), None, None),
        P(("expert", "dp"), None, None),
        P("expert", "dp", "tensor"),
        P("expert", "tensor", "dp"),
        P("expert", "tensor"),
        P("expert", "dp"),
    )
    return jax.shard_map(
        local,
        mesh=mesh,
        in_specs=placed,
        out_specs=(
            P(("expert", "dp"), "tensor"),
            P(("expert", "dp"), None, None),
            P("expert", "dp", "tensor"),
            P("expert", "tensor", "dp"),
            P("expert", "tensor"),
            P("expert", "dp"),
        ),
        check_vma=False,
    )
```

```python
import functools

import jax
import jax.numpy as jnp
from jax import lax
from jax.experimental import pallas as pl
from jax.experimental.pallas import tpu as pltpu
from jax.sharding import PartitionSpec as P

gelu_coeff = 0.7978845608028654
cubic_coeff = 0.044715

D = 1664
HALF = 896
MIB = 1 << 20
f32, bf16 = jnp.float32, jnp.bfloat16
VMEM = pl.BlockSpec(memory_space=pltpu.VMEM)
ANY = pl.BlockSpec(memory_space=pl.ANY)
GROUPS = (0, 1, 7, 2, 6, 3, 5, 4)
HALVES = (range(0, 4), range(4, 8))
FACTOR = 1024.0 ** -0.5


def where_am_i():
    e, d, t = lax.axis_index("expert"), lax.axis_index("dp"), lax.axis_index("tensor")
    y, zl = lax.div(e, 8), lax.rem(e, 8)
    zh, c = lax.div(t, 2), lax.rem(t, 2)
    return e, d, t, y, zl, zh, c


def neighbours():
    e, d, t, y, zl, zh, c = where_am_i()
    z = zh * 8 + zl

    def at(dy, dz):
        yy, zz = lax.rem(y + dy + 4, 4), lax.rem(z + dz + 16, 16)
        return (yy * 8 + lax.rem(zz, 8), d, lax.div(zz, 8) * 2 + c)

    def along(dx):
        return (e, lax.rem(d + dx, 4), t)

    return at, along, (e, d, t + 1 - 2 * c)


def greet(devices):
    barrier = pltpu.get_barrier_semaphore()
    for device in devices:
        pl.semaphore_signal(barrier, inc=1, device_id=device, device_id_type=pl.DeviceIdType.MESH)
    return lambda: pl.semaphore_wait(barrier, len(devices))


def remote(src, dst, send, recv, device):
    return pltpu.make_async_remote_copy(
        src_ref=src, dst_ref=dst, send_sem=send, recv_sem=recv,
        device_id=device, device_id_type=pl.DeviceIdType.MESH,
    )


def gelu_parts(hidden):
    inner_arg = gelu_coeff * (hidden + cubic_coeff * hidden * hidden * hidden)
    tangent = jnp.tanh(inner_arg)
    output = 0.5 * hidden * (1.0 + tangent)
    gelu_slope = 0.5 * (1.0 + tangent) + 0.5 * hidden * (1.0 - tangent * tangent) * gelu_coeff * (
        1.0 + 3.0 * cubic_coeff * hidden * hidden
    )
    return output, gelu_slope


def window(full, d):
    wide = full[:, 384 * d : 384 * d + 512]
    return pltpu.roll(wide, 512 - 32 * d, 1) if d else wide


def tn(a, b):
    return lax.dot_general(a, b, (((0,), (0,)), ((), ())), preferred_element_type=f32)


def nt(a, b):
    return lax.dot_general(a, b, (((1,), (1,)), ((), ())), preferred_element_type=f32)


def kernel(
    tokens_hbm, grads_hbm, picks, gates, w_in, w_out, s_in, s_out,
    gt, gg, gw_in, gw_out, gs_in, gs_out,
    tokens, grads, onehot, stage, xg, win, wout, so,
    q_in, t_in, q_out, t_out, so_col, p_in, p_out,
    xs, ys, act, hid, gwin, gwout, gsin, gsout,
    dxs, dxg, cbuf, cgate, sbuf, sgate, vbuf, xbuf, xgate, pair, rbuf, rb, obuf, tbuf, tsum,
    local_sem, w_send, w_recv, a_send, a_recv, x_send, x_recv, f_send, f_recv, p_send, p_recv,
    c_send, c_recv, s_send, s_recv, g_send, g_recv, r_send, r_recv, t_send, t_recv,
):
    e, d, t, y, zl, zh, c = where_am_i()
    at, along, partner = neighbours()
    over, cross = at(0, 8), (e, d, 3 - t)
    mine = pl.ds(pl.multiple_of(d * 256, 256), 256)

    fetch = [
        pltpu.make_async_copy(tokens_hbm, tokens, local_sem.at[0]),
        pltpu.make_async_copy(grads_hbm, grads, local_sem.at[1]),
        pltpu.make_async_copy(w_in.at[:, mine], win.at[d], local_sem.at[2]),
        pltpu.make_async_copy(w_out.at[:, mine], wout.at[d], local_sem.at[3]),
        pltpu.make_async_copy(s_out, so.at[d], local_sem.at[4]),
    ]
    for copy in fetch:
        copy.start()
    all_in = greet(
        [along(dx) for dx in (1, 2, 3)]
        + [partner, cross]
        + [at(dy, dz) for dz in range(16) for dy in range(4) if (dy, dz) != (0, 0)]
    )

    lane = lax.broadcasted_iota(jnp.int32, (8, 128), 1)
    gates32 = gates[...].astype(f32)
    onehot[...] = jnp.concatenate(
        [(lane == picks[:, k : k + 1]).astype(f32) for k in range(32)], axis=0
    ).astype(bf16)
    gate_tile = jnp.concatenate(
        [jnp.broadcast_to(gates32[:, k : k + 1], (8, 128)) for k in range(32)], axis=0
    )
    body = pl.ds(pl.multiple_of(c * HALF, 128), HALF - 128)

    def rows(ref):
        most = jnp.dot(onehot[...], ref[:, body], preferred_element_type=f32)
        last = jnp.dot(onehot[...], ref[:, HALF - 128 : HALF], preferred_element_type=f32)
        last = jnp.where(c == 0, last, gate_tile)
        return most.reshape(32, 8, HALF - 128), last.reshape(32, 8, 128)

    fetch[0].wait()
    fetch[1].wait()
    x_most, x_last = rows(tokens)
    g_most, g_last = rows(grads)
    stage[:, :, 0 : HALF - 128] = jnp.concatenate([x_most, g_most], axis=1).astype(bf16)
    stage[:, :, HALF - 128 : HALF] = jnp.concatenate([x_last, g_last], axis=1).astype(bf16)

    all_in()

    w_copies = []
    for dx in (1, 3, 2):
        there = lax.rem(d + dx, 4)
        cols = pl.ds(pl.multiple_of(there * 256, 256), 256)
        for k, (src, dst) in enumerate(
            ((w_in.at[:, cols], win.at[d]), (w_out.at[:, cols], wout.at[d]), (s_out, so.at[d]))
        ):
            copy = remote(src, dst, w_send.at[k, dx - 1], w_recv.at[k, dx - 1], along(dx))
            copy.start()
            w_copies.append(copy)

    own = pltpu.make_async_copy(stage.at[e], xg.at[0, c, 0], local_sem.at[5])
    own.start()
    for p, dz in enumerate(GROUPS):
        for dy in range(4):
            if (dy, dz) == (0, 0):
                continue
            way = dz if dz < 4 else dz - 8
            if dz == 4:
                way = 4 if dy < 2 else -4
            device = at(dy, way)
            remote(
                stage.at[device[0]], xg.at[0, c, p * 4 + dy], a_send.at[p], a_recv.at[p], device
            ).start()

    def part(block, g):
        return xg.at[block, c, pl.ds(4 * g, 4)]

    def to_partner(block, g):
        return remote(part(block, g), part(block, g), p_send.at[block, g], p_recv.at[block, g], partner)

    def forth(g):
        return remote(part(0, g), part(1, g), x_send.at[0, g], x_recv.at[0, g], along(1))

    def back(g):
        return remote(part(0, g), part(3, g), x_send.at[1, g], x_recv.at[1, g], along(3))

    def onward(g):
        if g % 2 == 0:
            return remote(part(1, g), part(2, g), f_send.at[g], f_recv.at[g], along(1))
        return remote(part(3, g), part(2, g), f_send.at[g], f_recv.at[g], along(3))

    def arrived(g):
        n = 3 if g == 0 else 4
        ref = xg.at[0, c, pl.ds(4 * g + 4 - n, n)]
        return remote(ref, ref, a_send.at[g], a_recv.at[g], partner)

    own.wait()
    for g in range(8):
        arrived(g).wait_recv()
        forth(g).start()
        back(g).start()
        to_partner(0, g).start()

    for copy in fetch[2:]:
        copy.wait()
    for copy in w_copies:
        copy.wait_recv()
    scale_in = s_in[:, mine]
    inv_in = 1.0 / scale_in
    for b in range(4):
        part_rows = slice(416 * b, 416 * b + 416)
        tangent = jnp.tanh(win[b].astype(f32) * inv_in)
        t_in[part_rows] = tangent
        q_in[part_rows] = (scale_in * tangent).astype(bf16)
        wide = jnp.concatenate([so[b], jnp.ones((1, 96), f32)], axis=1)
        col = jnp.broadcast_to(wide, (128, 512)).T[:416]
        so_col[part_rows] = col
        col = jnp.concatenate([col, col], axis=1)
        tangent = jnp.tanh(wout[b].astype(f32) * (1.0 / col))
        t_out[part_rows] = tangent
        q_out[part_rows] = (col * tangent).astype(bf16)

    c_copies = [
        [
            (
                remote(dxs.at[h, j, 1 - c], cbuf.at[h, j], c_send.at[0, h, j], c_recv.at[0, h, j], partner),
                remote(dxg.at[h, j], cgate.at[h, j], c_send.at[1, h, j], c_recv.at[1, h, j], partner),
            )
            for j in range(4)
        ]
        for h in range(2)
    ]
    gate_copies = [
        [
            remote(sgate.at[h, j - 1], xgate.at[h, j - 1], s_send.at[h, j - 1], s_recv.at[h, j - 1], along(4 - j))
            for j in (1, 2, 3)
        ]
        for h in range(2)
    ]
    ahead = [along(1), along(3)]
    rows32 = [pl.ds(0, 32), pl.ds(32, 32)]
    via = [
        [
            remote(sbuf.at[h, 1, rows32[k]], vbuf.at[h, k], s_send.at[h, 3 + k], s_recv.at[h, 3 + k], ahead[k])
            for k in range(2)
        ]
        for h in range(2)
    ]

    def to_side(h, k, rows, sem):
        return remote(
            sbuf.at[h, 2 - 2 * k, rows], xbuf.at[h, k, rows], s_send.at[h, sem], s_recv.at[h, sem], ahead[k]
        )

    alone = [[to_side(h, k, rows32[1 - k], 5 + k) for k in range(2)] for h in range(2)]
    joint = [[to_side(h, k, rows32[k], 7 + k) for k in range(2)] for h in range(2)]

    def forward(h, j):
        for g in HALVES[h]:
            to_partner(j, g).wait_recv()
        blocks, at_rows = pl.ds(16 * h, 16), slice(128 * h, 128 * h + 128)
        low, high = xg[j, 0, blocks].astype(f32), xg[j, 1, blocks].astype(f32)

        def rows_of(k):
            pick = slice(8 * k, 8 * k + 8)
            left = low[:, pick].reshape(128, HALF)
            right = high[:, pick].reshape(128, HALF)
            return jnp.concatenate([left, right[:, : HALF - 128]], axis=1), right[:, HALF - 128 :]

        x, gate_rows = rows_of(0)
        g, _ = rows_of(1)
        x = x.astype(bf16)
        xs[j, at_rows] = x
        gate = gate_rows[:, 0:1]
        ys[j, at_rows] = (gate * g).astype(bf16)
        hidden = jnp.dot(x, q_in[...], preferred_element_type=f32)
        value, slope = gelu_parts(hidden)
        value = value.astype(bf16)
        act[j, at_rows] = value
        back_prop = jnp.dot(g.astype(bf16), q_out[...], preferred_element_type=f32)
        gate_part = jnp.sum(value.astype(f32) * back_prop, axis=1, keepdims=True)
        hidden_grad = (gate * back_prop * slope).astype(bf16)
        hid[j, at_rows] = hidden_grad
        dx = nt(hidden_grad, q_in[...])
        dxs[h, j] = dx.astype(bf16).reshape(2, 64, D)
        compact = jnp.zeros((8, 128), f32)
        for k in range(16):
            compact = jnp.where(lane == k, gate_part[8 * k : 8 * k + 8], compact)
        dxg[h, j] = compact
        for copy in c_copies[h][j]:
            copy.start()

    def weigh(j):
        into_in, into_out = tn(xs[j], hid[j]), tn(ys[j], act[j])
        if j:
            into_in, into_out = p_in[...] + into_in, p_out[...] + into_out
        p_in[...] = into_in
        p_out[...] = into_out

    def hand_over(h, j):
        for copy in c_copies[h][j]:
            copy.wait_recv()
        sbuf[h, j - 1] = (dxs[h, j, c].astype(f32) + cbuf[h, j].astype(f32)).astype(bf16)
        sgate[h, j - 1] = dxg[h, j] + cgate[h, j]
        gate_copies[h][j - 1].start()
        if j == 2:
            for copy in via[h]:
                copy.start()
        else:
            alone[h][0 if j == 3 else 1].start()

    def join(h):
        for k in range(2):
            via[h][k].wait_recv()
            rows = slice(32 * k, 32 * k + 32)
            sbuf[h, 2 - 2 * k, rows] = (
                sbuf[h, 2 - 2 * k, rows].astype(f32) + vbuf[h, k].astype(f32)
            ).astype(bf16)
            joint[h][k].start()

    def give_back(h):
        for copy in c_copies[h][0]:
            copy.wait_recv()
        for copy in gate_copies[h] + alone[h] + joint[h]:
            copy.wait_recv()
        total = (
            dxs[h, 0, c].astype(f32)
            + cbuf[h, 0].astype(f32)
            + xbuf[h, 0].astype(f32)
            + xbuf[h, 1].astype(f32)
        )
        gates_sum = dxg[h, 0] + cgate[h, 0] + xgate[h, 0] + xgate[h, 1] + xgate[h, 2]
        gates_sum = jnp.where(c == 0, gates_sum, pltpu.roll(gates_sum, 120, 1))
        gate_col = jnp.concatenate(
            [jnp.broadcast_to(gates_sum[:, k : k + 1], (8, 128)) for k in range(8)], axis=0
        )
        top = gate_col.astype(bf16).astype(f32)
        rest = gate_col - top
        first = lax.broadcasted_iota(jnp.int32, (64, 128), 1)
        extra = jnp.where(first == 32, top, rest)
        own_blocks = pl.ds(pl.multiple_of(16 * h + c * 8, 8), 8)
        for k in range(4):
            piece = window(total, k)
            last = jnp.where((first == 32) | (first == 33), extra, piece[:, 384:])
            piece = jnp.concatenate([piece[:, :384], last], axis=1).reshape(8, 8, 512)
            piece = jnp.concatenate([piece[:, :, :256], piece[:, :, 256:]], axis=1).astype(bf16)
            pair[h, k % 2, k // 2] = piece
        swap = remote(
            pair.at[h, 1 - c], rbuf.at[:, own_blocks], r_send.at[2 + h], r_recv.at[2 + h], partner
        )
        swap.start()
        rbuf[:, own_blocks] = pair[h, c]
        swap.wait_recv()
        if h == 0:
            keep.start()
        for p in HALVES[h]:
            for over_z in (8, 0):
                for dy in range(4):
                    dz = GROUPS[p] + over_z
                    if (dy, dz) == (0, 0):
                        continue
                    device = at(-dy, -dz)
                    remote(
                        rbuf.at[lax.div(device[2], 2), p * 4 + dy], rb.at[zh, e],
                        r_send.at[h], r_recv.at[h], device,
                    ).start()
        return swap

    keep = pltpu.make_async_copy(rbuf.at[zh, 0], rb.at[zh, e], local_sem.at[6])

    def pass_on(h):
        for g in HALVES[h]:
            forth(g).wait_recv()
            back(g).wait_recv()
            onward(g).start()
            to_partner(1, g).start()
            to_partner(3, g).start()

    def last_block(h):
        for g in HALVES[h]:
            onward(g).wait_recv()
            to_partner(2, g).start()

    forward(0, 0)
    forward(1, 0)
    pass_on(0)
    weigh(0)
    forward(0, 1)
    forward(0, 3)
    hand_over(0, 1)
    pass_on(1)
    hand_over(0, 3)
    last_block(0)
    forward(1, 1)
    weigh(1)
    forward(0, 2)
    forward(1, 3)
    hand_over(0, 2)
    hand_over(1, 1)
    weigh(3)
    hand_over(1, 3)
    last_block(1)
    join(0)
    forward(1, 2)
    swaps = [give_back(0)]
    hand_over(1, 2)
    weigh(2)
    join(1)

    total_s = jnp.zeros((1, 256), f32)
    for b in range(4):
        part_rows = slice(416 * b, 416 * b + 416)
        total = p_in[part_rows] * FACTOR
        tangent = t_in[part_rows]
        sech = 1.0 - tangent * tangent
        gwin[b] = (total * sech).astype(bf16)
        scaled = win[b].astype(f32) * inv_in
        total_s += jnp.sum(total * (tangent - scaled * sech), axis=0, keepdims=True)
        total = p_out[part_rows] * FACTOR
        tangent = t_out[part_rows]
        sech = 1.0 - tangent * tangent
        gwout[b] = (total * sech).astype(bf16)
        inv = 1.0 / so_col[part_rows]
        scaled = wout[b].astype(f32) * jnp.concatenate([inv, inv], axis=1)
        terms = total * (tangent - scaled * sech)
        terms = terms[:, :128] + terms[:, 128:]
        terms = jnp.concatenate([terms, jnp.zeros((96, 128), f32)], axis=0)
        gsout[b] = jnp.sum(terms.T, axis=0, keepdims=True)
    gsin[...] = total_s

    g_copies = []
    for k, (src, dst) in enumerate((
        (gsout, obuf.at[d]),
        (gsin, gs_in.at[d]),
        (gwin, gw_in.at[:, mine]),
        (gwout, gw_out.at[:, mine]),
    )):
        for dx in (1, 3, 2):
            block = src if k == 1 else src.at[lax.rem(d + dx, 4)]
            copy = remote(block, dst, g_send.at[k, dx - 1], g_recv.at[k, dx - 1], along(dx))
            copy.start()
            g_copies.append(copy)
    stay = [
        pltpu.make_async_copy(gsout.at[d], obuf.at[d], local_sem.at[7]),
        pltpu.make_async_copy(gsin, gs_in.at[d], local_sem.at[8]),
        pltpu.make_async_copy(gwin.at[d], gw_in.at[:, mine], local_sem.at[9]),
        pltpu.make_async_copy(gwout.at[d], gw_out.at[:, mine], local_sem.at[10]),
    ]
    for copy in stay:
        copy.start()

    swaps.append(give_back(1))

    stay[0].wait()
    for copy in g_copies[:3]:
        copy.wait_recv()
    tsum[...] = obuf[0] + obuf[1] + obuf[2] + obuf[3]
    t_copies = []
    for k, device in enumerate((partner, over, cross)):
        copy = remote(tsum, tbuf.at[k], t_send.at[k], t_recv.at[k], device)
        copy.start()
        t_copies.append(copy)
    for copy in t_copies:
        copy.wait_recv()
    gs_out[...] = (tsum[...] + tbuf[0] + tbuf[1] + tbuf[2])[:, :416]

    keep.wait()
    for h, count in ((0, 31), (1, 32)):
        returned = rbuf.at[0, pl.ds(0, count)]
        remote(returned, returned, r_send.at[h], r_recv.at[h], partner).wait()
    left = jnp.zeros((256, 128), f32)
    right = jnp.zeros((256, 128), f32)
    gate = jnp.zeros((256, 128), f32)
    for h in range(2):
        got = rb[h].astype(f32)
        lo = got[:, :8].reshape(256, 256)
        hi = got[:, 8:].reshape(256, 256)
        left += tn(lo.astype(bf16), onehot[...])
        right += tn(hi.astype(bf16), onehot[...])
        gate += hi[:, 128:]
    gt[0:256] = left.astype(bf16)
    gt[256:416] = right[:160].astype(bf16)
    gates_out = jnp.zeros((8, 128), f32)
    for k in range(32):
        rows8 = gate[8 * k : 8 * k + 8]
        gates_out = jnp.where(lane == k, rows8[:, 32:33] + rows8[:, 33:34], gates_out)
    gg[...] = gates_out[:, :32]

    for g in range(8):
        arrived(g).wait_send()
        forth(g).wait_send()
        back(g).wait_send()
        onward(g).wait_send()
        for block in range(4):
            to_partner(block, g).wait_send()
    for copy in w_copies + t_copies + g_copies + swaps:
        copy.wait_send()
    for h in range(2):
        for copy in via[h] + alone[h] + joint[h] + gate_copies[h]:
            copy.wait_send()
        for pair_of in c_copies[h]:
            for copy in pair_of:
                copy.wait_send()
    for copy in g_copies[3:]:
        copy.wait_recv()
    for copy in stay[1:]:
        copy.wait()


DMA = pltpu.SemaphoreType.DMA


def struct(*shape, dtype=bf16):
    return jax.ShapeDtypeStruct(shape, dtype)


def settle(*refs):
    ins, outs, held, sems = refs[:6], refs[6:12], refs[12:18], refs[18]
    first = [pltpu.make_async_copy(ins[k], held[k], sems.at[0, k]) for k in range(6)]
    then = [pltpu.make_async_copy(held[k], outs[k], sems.at[1, k]) for k in range(6)]
    for copy in first:
        copy.start()
    for k in range(6):
        first[k].wait()
        then[k].start()
    for copy in then:
        copy.wait()


def local(tokens, grad_out, picks, gates, w_in, w_out, scale_in, scale_out):
    shapes = (
        struct(416, 128),
        struct(8, 32, dtype=f32),
        struct(416, 1024),
        struct(416, 1024),
        struct(4, 1, 256, dtype=f32),
        struct(1, 416, dtype=f32),
    )
    results = pl.pallas_call(
        kernel,
        out_shape=shapes,
        in_specs=[ANY, ANY, VMEM, VMEM, ANY, ANY, VMEM, VMEM],
        out_specs=(VMEM, VMEM, ANY, ANY, VMEM, VMEM),
        scratch_shapes=[
            pltpu.VMEM((128, D), bf16),
            pltpu.VMEM((128, D), bf16),
            pltpu.VMEM((256, 128), bf16),
            pltpu.VMEM((32, 16, HALF), bf16),
            pltpu.VMEM((4, 2, 32, 16, HALF), bf16),
            pltpu.VMEM((4, 416, 256), bf16),
            pltpu.VMEM((4, 416, 256), bf16),
            pltpu.VMEM((4, 1, 416), f32),
            pltpu.VMEM((D, 256), bf16),
            pltpu.VMEM((D, 256), f32),
            pltpu.VMEM((D, 256), bf16),
            pltpu.VMEM((D, 256), f32),
            pltpu.VMEM((D, 128), f32),
            pltpu.VMEM((D, 256), f32),
            pltpu.VMEM((D, 256), f32),
            pltpu.VMEM((4, 256, D), bf16),
            pltpu.VMEM((4, 256, D), bf16),
            pltpu.VMEM((4, 256, 256), bf16),
            pltpu.VMEM((4, 256, 256), bf16),
            pltpu.VMEM((4, 416, 256), bf16),
            pltpu.VMEM((4, 416, 256), bf16),
            pltpu.VMEM((1, 256), f32),
            pltpu.VMEM((4, 1, 512), f32),
            pltpu.VMEM((2, 4, 2, 64, D), bf16),
            pltpu.VMEM((2, 4, 8, 128), f32),
            pltpu.VMEM((2, 4, 64, D), bf16),
            pltpu.VMEM((2, 4, 8, 128), f32),
            pltpu.VMEM((2, 3, 64, D), bf16),
            pltpu.VMEM((2, 3, 8, 128), f32),
            pltpu.VMEM((2, 2, 32, D), bf16),
            pltpu.VMEM((2, 2, 64, D), bf16),
            pltpu.VMEM((2, 3, 8, 128), f32),
            pltpu.VMEM((2, 2, 2, 8, 16, 256), bf16),
            pltpu.VMEM((2, 32, 16, 256), bf16),
            pltpu.VMEM((2, 32, 16, 256), bf16),
            pltpu.VMEM((4, 1, 512), f32),
            pltpu.VMEM((3, 1, 512), f32),
            pltpu.VMEM((1, 512), f32),
            DMA((11,)),
            DMA((3, 3)), DMA((3, 3)),
            DMA((8,)), DMA((8,)),
            DMA((2, 8)), DMA((2, 8)),
            DMA((8,)), DMA((8,)),
            DMA((4, 8)), DMA((4, 8)),
            DMA((2, 2, 4)), DMA((2, 2, 4)),
            DMA((2, 9)), DMA((2, 9)),
            DMA((4, 3)), DMA((4, 3)),
            DMA((4,)), DMA((4,)),
            DMA((3,)), DMA((3,)),
        ],
        compiler_params=pltpu.CompilerParams(
            collective_id=0, has_side_effects=True, vmem_limit_bytes=58 * MIB
        ),
        name="moe_backward",
    )(
        tokens, grad_out, picks[0].T, gates[0].T, w_in[0], w_out[0].T, scale_in, scale_out,
    )
    gt, gg, gw_in, gw_out, gs_in, gs_out = pl.pallas_call(
        settle,
        out_shape=shapes,
        in_specs=[ANY] * 6,
        out_specs=(ANY,) * 6,
        scratch_shapes=[pltpu.VMEM(o.shape, o.dtype) for o in shapes] + [DMA((2, 6))],
        name="settle",
    )(*results)
    return gt.T, gg.T[None], gw_in[None], gw_out.T[None], gs_in.reshape(1, 1024), gs_out


def solution(mesh):
    placed = (
        P(("expert", "dp"), None),
        P(("expert", "dp"), None),
        P(("expert", "dp"), None, None),
        P(("expert", "dp"), None, None),
        P("expert", "dp", "tensor"),
        P("expert", "tensor", "dp"),
        P("expert", "tensor"),
        P("expert", "dp"),
    )
    return jax.shard_map(
        local,
        mesh=mesh,
        in_specs=placed,
        out_specs=(
            P(("expert", "dp"), "tensor"),
            P(("expert", "dp"), None, None),
            P("expert", "dp", "tensor"),
            P("expert", "tensor", "dp"),
            P("expert", "tensor"),
            P("expert", "dp"),
        ),
        check_vma=False,
    )
```

```python
import functools

import jax
import jax.numpy as jnp
from jax import lax
from jax.experimental import pallas as pl
from jax.experimental.pallas import tpu as pltpu
from jax.sharding import PartitionSpec as P

gelu_coeff = 0.7978845608028654
cubic_coeff = 0.044715

D = 1664
HALF = 896
MIB = 1 << 20
f32, bf16 = jnp.float32, jnp.bfloat16
VMEM = pl.BlockSpec(memory_space=pltpu.VMEM)
ANY = pl.BlockSpec(memory_space=pl.ANY)
GROUPS = (0, 1, 7, 2, 6, 3, 5, 4)
HALVES = (range(0, 4), range(4, 8))
FACTOR = 1024.0 ** -0.5


def where_am_i():
    e, d, t = lax.axis_index("expert"), lax.axis_index("dp"), lax.axis_index("tensor")
    y, zl = lax.div(e, 8), lax.rem(e, 8)
    zh, c = lax.div(t, 2), lax.rem(t, 2)
    return e, d, t, y, zl, zh, c


def neighbours():
    e, d, t, y, zl, zh, c = where_am_i()
    z = zh * 8 + zl

    def at(dy, dz):
        yy, zz = lax.rem(y + dy + 4, 4), lax.rem(z + dz + 16, 16)
        return (yy * 8 + lax.rem(zz, 8), d, lax.div(zz, 8) * 2 + c)

    def along(dx):
        return (e, lax.rem(d + dx, 4), t)

    return at, along, (e, d, t + 1 - 2 * c)


def greet(devices):
    barrier = pltpu.get_barrier_semaphore()
    for device in devices:
        pl.semaphore_signal(barrier, inc=1, device_id=device, device_id_type=pl.DeviceIdType.MESH)
    return lambda: pl.semaphore_wait(barrier, len(devices))


def remote(src, dst, send, recv, device):
    return pltpu.make_async_remote_copy(
        src_ref=src, dst_ref=dst, send_sem=send, recv_sem=recv,
        device_id=device, device_id_type=pl.DeviceIdType.MESH,
    )


def gelu_parts(hidden):
    inner_arg = gelu_coeff * (hidden + cubic_coeff * hidden * hidden * hidden)
    tangent = jnp.tanh(inner_arg)
    output = 0.5 * hidden * (1.0 + tangent)
    gelu_slope = 0.5 * (1.0 + tangent) + 0.5 * hidden * (1.0 - tangent * tangent) * gelu_coeff * (
        1.0 + 3.0 * cubic_coeff * hidden * hidden
    )
    return output, gelu_slope


def window(full, d):
    wide = full[:, 384 * d : 384 * d + 512]
    return pltpu.roll(wide, 512 - 32 * d, 1) if d else wide


def tn(a, b):
    return lax.dot_general(a, b, (((0,), (0,)), ((), ())), preferred_element_type=f32)


def nt(a, b):
    return lax.dot_general(a, b, (((1,), (1,)), ((), ())), preferred_element_type=f32)


def kernel(
    tokens_hbm, grads_hbm, picks, gates, w_in, w_out, s_in, s_out,
    gt, gg, gw_in, gw_out, gs_in, gs_out,
    tokens, grads, onehot, stage_0, stage_1, xg_0, xg_1, win, wout, so,
    q_in, t_in, q_out, t_out, so_col, p_in, p_out,
    xs, ys, act, hid, gwin, gwout, gsin, gsout,
    dxs, dxg, cbuf, cgate, sbuf, sgate, vbuf, xbuf, xgate, pair, rbuf, rb, obuf, tbuf, tsum,
    local_sem, w_send, w_recv, a_send, a_recv, x_send, x_recv, f_send, f_recv, p_send, p_recv,
    c_send, c_recv, s_send, s_recv, g_send, g_recv, r_send, r_recv, t_send, t_recv,
):
    e, d, t, y, zl, zh, c = where_am_i()
    at, along, partner = neighbours()
    over, cross = at(0, 8), (e, d, 3 - t)
    mine = pl.ds(pl.multiple_of(d * 256, 256), 256)
    stage, xg = (stage_0, stage_1), (xg_0, xg_1)
    columns = (slice(0, HALF), slice(HALF, D))

    def by_core(step):
        for q in range(2):
            pl.when(c == q)(functools.partial(step, q))

    fetch = [
        pltpu.make_async_copy(tokens_hbm, tokens, local_sem.at[0]),
        pltpu.make_async_copy(grads_hbm, grads, local_sem.at[1]),
        pltpu.make_async_copy(w_in.at[:, mine], win.at[d], local_sem.at[2]),
        pltpu.make_async_copy(w_out.at[:, mine], wout.at[d], local_sem.at[3]),
        pltpu.make_async_copy(s_out, so.at[d], local_sem.at[4]),
    ]
    for copy in fetch:
        copy.start()
    all_in = greet(
        [along(dx) for dx in (1, 2, 3)]
        + [partner, cross]
        + [at(dy, dz) for dz in range(16) for dy in range(4) if (dy, dz) != (0, 0)]
    )

    lane = lax.broadcasted_iota(jnp.int32, (8, 128), 1)
    gates32 = gates[...].astype(f32)
    onehot[...] = jnp.concatenate(
        [(lane == picks[:, k : k + 1]).astype(f32) for k in range(32)], axis=0
    ).astype(bf16)
    gate_col = jnp.concatenate([gates32[:, k : k + 1] for k in range(32)], axis=0)
    fetch[0].wait()
    fetch[1].wait()

    def gather(q):
        x = jnp.dot(onehot[...], tokens[:, columns[q]], preferred_element_type=f32)
        g = jnp.dot(onehot[...], grads[:, columns[q]], preferred_element_type=f32)
        width = x.shape[1]
        rows = [x.reshape(32, 8, width), (gate_col * g).reshape(32, 8, width)]
        stage[q][...] = jnp.concatenate(rows, axis=1).astype(bf16)

    by_core(gather)
    all_in()

    w_copies = []
    for dx in (1, 3, 2):
        there = lax.rem(d + dx, 4)
        cols = pl.ds(pl.multiple_of(there * 256, 256), 256)
        for k, (src, dst) in enumerate(
            ((w_in.at[:, cols], win.at[d]), (w_out.at[:, cols], wout.at[d]), (s_out, so.at[d]))
        ):
            copy = remote(src, dst, w_send.at[k, dx - 1], w_recv.at[k, dx - 1], along(dx))
            copy.start()
            w_copies.append(copy)

    def own(q):
        return pltpu.make_async_copy(stage[q].at[e], xg[q].at[0, 0], local_sem.at[5])

    def dispatch(q):
        own(q).start()
        for p, dz in enumerate(GROUPS):
            for dy in range(4):
                if (dy, dz) == (0, 0):
                    continue
                way = dz if dz < 4 else dz - 8
                if dz == 4:
                    way = 4 if dy < 2 else -4
                device = at(dy, way)
                remote(
                    stage[q].at[device[0]], xg[q].at[0, p * 4 + dy], a_send.at[p], a_recv.at[p], device
                ).start()

    by_core(dispatch)

    def part(q, block, g):
        return xg[q].at[block, pl.ds(4 * g, 4)]

    def to_partner(q, block, g):
        ref = part(q, block, g)
        return remote(ref, ref, p_send.at[block, g], p_recv.at[block, g], partner)

    def forth(q, g):
        return remote(part(q, 0, g), part(q, 1, g), x_send.at[0, g], x_recv.at[0, g], along(1))

    def back(q, g):
        return remote(part(q, 0, g), part(q, 3, g), x_send.at[1, g], x_recv.at[1, g], along(3))

    def onward(q, g):
        if g % 2 == 0:
            return remote(part(q, 1, g), part(q, 2, g), f_send.at[g], f_recv.at[g], along(1))
        return remote(part(q, 3, g), part(q, 2, g), f_send.at[g], f_recv.at[g], along(3))

    def arrived(q, g):
        n = 3 if g == 0 else 4
        ref = xg[q].at[0, pl.ds(4 * g + 4 - n, n)]
        return remote(ref, ref, a_send.at[g], a_recv.at[g], partner)

    def first_blocks(q):
        own(q).wait()
        for g in range(8):
            arrived(q, g).wait_recv()
            to_partner(q, 0, g).start()
            if g < 4:
                forth(q, g).start()
                back(q, g).start()

    by_core(first_blocks)

    for copy in fetch[2:]:
        copy.wait()
    for copy in w_copies:
        copy.wait_recv()
    scale_in = s_in[:, mine]
    inv_in = 1.0 / scale_in
    for b in range(4):
        part_rows = slice(416 * b, 416 * b + 416)
        tangent = jnp.tanh(win[b].astype(f32) * inv_in)
        t_in[part_rows] = tangent
        q_in[part_rows] = (scale_in * tangent).astype(bf16)
        wide = jnp.concatenate([so[b], jnp.ones((1, 96), f32)], axis=1)
        col = jnp.broadcast_to(wide, (128, 512)).T[:416]
        so_col[part_rows] = col
        col = jnp.concatenate([col, col], axis=1)
        tangent = jnp.tanh(wout[b].astype(f32) * (1.0 / col))
        t_out[part_rows] = tangent
        q_out[part_rows] = (col * tangent).astype(bf16)

    c_copies = [
        [
            (
                remote(dxs.at[h, j, 1 - c], cbuf.at[h, j], c_send.at[0, h, j], c_recv.at[0, h, j], partner),
                remote(dxg.at[h, j], cgate.at[h, j], c_send.at[1, h, j], c_recv.at[1, h, j], partner),
            )
            for j in range(4)
        ]
        for h in range(2)
    ]
    gate_copies = [
        [
            remote(sgate.at[h, j - 1], xgate.at[h, j - 1], s_send.at[h, j - 1], s_recv.at[h, j - 1], along(4 - j))
            for j in (1, 2, 3)
        ]
        for h in range(2)
    ]
    ahead = [along(1), along(3)]
    rows32 = [pl.ds(0, 32), pl.ds(32, 32)]
    via = [
        [
            remote(sbuf.at[h, 1, rows32[k]], vbuf.at[h, k], s_send.at[h, 3 + k], s_recv.at[h, 3 + k], ahead[k])
            for k in range(2)
        ]
        for h in range(2)
    ]

    def to_side(h, k, rows, sem):
        return remote(
            sbuf.at[h, 2 - 2 * k, rows], xbuf.at[h, k, rows], s_send.at[h, sem], s_recv.at[h, sem], ahead[k]
        )

    alone = [[to_side(h, k, rows32[1 - k], 5 + k) for k in range(2)] for h in range(2)]
    joint = [[to_side(h, k, rows32[k], 7 + k) for k in range(2)] for h in range(2)]

    def forward(h, j):
        def from_partner(q):
            for g in HALVES[h]:
                to_partner(1 - q, j, g).wait_recv()

        by_core(from_partner)
        blocks, at_rows = pl.ds(16 * h, 16), slice(128 * h, 128 * h + 128)
        low, high = xg_0[j, blocks].astype(f32), xg_1[j, blocks].astype(f32)

        def rows_of(k):
            pick = slice(8 * k, 8 * k + 8)
            left = low[:, pick].reshape(128, HALF)
            right = high[:, pick].reshape(128, D - HALF)
            return jnp.concatenate([left, right], axis=1).astype(bf16)

        x, g = rows_of(0), rows_of(1)
        xs[j, at_rows] = x
        ys[j, at_rows] = g
        hidden = jnp.dot(x, q_in[...], preferred_element_type=f32)
        value, slope = gelu_parts(hidden)
        value = value.astype(bf16)
        act[j, at_rows] = value
        back_prop = jnp.dot(g, q_out[...], preferred_element_type=f32)
        gate_part = jnp.sum(value.astype(f32) * back_prop, axis=1, keepdims=True)
        hidden_grad = (back_prop * slope).astype(bf16)
        hid[j, at_rows] = hidden_grad
        dx = nt(hidden_grad, q_in[...])
        dxs[h, j] = dx.astype(bf16).reshape(2, 64, D)
        compact = jnp.zeros((8, 128), f32)
        for k in range(16):
            compact = jnp.where(lane == k, gate_part[8 * k : 8 * k + 8], compact)
        dxg[h, j] = compact
        for copy in c_copies[h][j]:
            copy.start()

    def weigh(j):
        into_in, into_out = tn(xs[j], hid[j]), tn(ys[j], act[j])
        if j:
            into_in, into_out = p_in[...] + into_in, p_out[...] + into_out
        p_in[...] = into_in
        p_out[...] = into_out

    def hand_over(h, j):
        for copy in c_copies[h][j]:
            copy.wait_recv()
        sbuf[h, j - 1] = (dxs[h, j, c].astype(f32) + cbuf[h, j].astype(f32)).astype(bf16)
        sgate[h, j - 1] = dxg[h, j] + cgate[h, j]
        gate_copies[h][j - 1].start()
        if j == 2:
            for copy in via[h]:
                copy.start()
        else:
            alone[h][0 if j == 3 else 1].start()

    def join(h):
        for k in range(2):
            via[h][k].wait_recv()
            rows = slice(32 * k, 32 * k + 32)
            sbuf[h, 2 - 2 * k, rows] = (
                sbuf[h, 2 - 2 * k, rows].astype(f32) + vbuf[h, k].astype(f32)
            ).astype(bf16)
            joint[h][k].start()

    def give_back(h):
        for copy in c_copies[h][0]:
            copy.wait_recv()
        for copy in gate_copies[h] + alone[h] + joint[h]:
            copy.wait_recv()
        total = (
            dxs[h, 0, c].astype(f32)
            + cbuf[h, 0].astype(f32)
            + xbuf[h, 0].astype(f32)
            + xbuf[h, 1].astype(f32)
        )
        gates_sum = dxg[h, 0] + cgate[h, 0] + xgate[h, 0] + xgate[h, 1] + xgate[h, 2]
        gates_sum = jnp.where(c == 0, gates_sum, pltpu.roll(gates_sum, 120, 1))
        gate_col = jnp.concatenate(
            [jnp.broadcast_to(gates_sum[:, k : k + 1], (8, 128)) for k in range(8)], axis=0
        )
        top = gate_col.astype(bf16).astype(f32)
        rest = gate_col - top
        first = lax.broadcasted_iota(jnp.int32, (64, 128), 1)
        extra = jnp.where(first == 32, top, rest)
        own_blocks = pl.ds(pl.multiple_of(16 * h + c * 8, 8), 8)
        for k in range(4):
            piece = window(total, k)
            last = jnp.where((first == 32) | (first == 33), extra, piece[:, 384:])
            piece = jnp.concatenate([piece[:, :384], last], axis=1).reshape(8, 8, 512)
            piece = jnp.concatenate([piece[:, :, :256], piece[:, :, 256:]], axis=1).astype(bf16)
            pair[h, k % 2, k // 2] = piece
        swap = remote(
            pair.at[h, 1 - c], rbuf.at[:, own_blocks], r_send.at[2 + h], r_recv.at[2 + h], partner
        )
        swap.start()
        rbuf[:, own_blocks] = pair[h, c]
        swap.wait_recv()
        if h == 0:
            keep.start()
        for p in HALVES[h]:
            for over_z in (8, 0):
                for dy in range(4):
                    dz = GROUPS[p] + over_z
                    if (dy, dz) == (0, 0):
                        continue
                    device = at(-dy, -dz)
                    remote(
                        rbuf.at[lax.div(device[2], 2), p * 4 + dy], rb.at[zh, e],
                        r_send.at[h], r_recv.at[h], device,
                    ).start()
        return swap

    keep = pltpu.make_async_copy(rbuf.at[zh, 0], rb.at[zh, e], local_sem.at[6])

    def pass_on(h):
        def step(q):
            for g in HALVES[h]:
                forth(q, g).wait_recv()
                back(q, g).wait_recv()
                onward(q, g).start()
                to_partner(q, 1, g).start()
                to_partner(q, 3, g).start()

        by_core(step)

    def last_block(h):
        def step(q):
            for g in HALVES[h]:
                onward(q, g).wait_recv()
                to_partner(q, 2, g).start()

        by_core(step)

    def remaining(lo, hi):
        def step(q):
            for g in range(lo, hi):
                forth(q, g).start()
                back(q, g).start()

        by_core(step)

    forward(0, 0)
    pass_on(0)
    remaining(4, 8)
    forward(1, 0)
    forward(0, 1)
    forward(0, 3)
    hand_over(0, 1)
    hand_over(0, 3)
    last_block(0)
    forward(0, 2)
    pass_on(1)
    hand_over(0, 2)
    forward(1, 1)
    forward(1, 3)
    join(0)
    hand_over(1, 1)
    weigh(0)
    weigh(1)
    weigh(3)
    last_block(1)
    forward(1, 2)
    hand_over(1, 3)
    hand_over(1, 2)
    swaps = [give_back(0)]
    weigh(2)

    total_s = jnp.zeros((1, 256), f32)
    for b in range(4):
        part_rows = slice(416 * b, 416 * b + 416)
        total = p_in[part_rows] * FACTOR
        tangent = t_in[part_rows]
        sech = 1.0 - tangent * tangent
        gwin[b] = (total * sech).astype(bf16)
        scaled = win[b].astype(f32) * inv_in
        total_s += jnp.sum(total * (tangent - scaled * sech), axis=0, keepdims=True)
        total = p_out[part_rows] * FACTOR
        tangent = t_out[part_rows]
        sech = 1.0 - tangent * tangent
        gwout[b] = (total * sech).astype(bf16)
        inv = 1.0 / so_col[part_rows]
        scaled = wout[b].astype(f32) * jnp.concatenate([inv, inv], axis=1)
        terms = total * (tangent - scaled * sech)
        terms = terms[:, :128] + terms[:, 128:]
        terms = jnp.concatenate([terms, jnp.zeros((96, 128), f32)], axis=0)
        gsout[b] = jnp.sum(terms.T, axis=0, keepdims=True)
    gsin[...] = total_s

    join(1)

    g_copies = []
    for k, (src, dst) in enumerate((
        (gsout, obuf.at[d]),
        (gsin, gs_in.at[d]),
        (gwin, gw_in.at[:, mine]),
        (gwout, gw_out.at[:, mine]),
    )):
        for dx in (1, 3, 2):
            block = src if k == 1 else src.at[lax.rem(d + dx, 4)]
            copy = remote(block, dst, g_send.at[k, dx - 1], g_recv.at[k, dx - 1], along(dx))
            copy.start()
            g_copies.append(copy)
    stay = [
        pltpu.make_async_copy(gsout.at[d], obuf.at[d], local_sem.at[7]),
        pltpu.make_async_copy(gsin, gs_in.at[d], local_sem.at[8]),
        pltpu.make_async_copy(gwin.at[d], gw_in.at[:, mine], local_sem.at[9]),
        pltpu.make_async_copy(gwout.at[d], gw_out.at[:, mine], local_sem.at[10]),
    ]
    for copy in stay:
        copy.start()

    swaps.append(give_back(1))

    stay[0].wait()
    for copy in g_copies[:3]:
        copy.wait_recv()
    tsum[...] = obuf[0] + obuf[1] + obuf[2] + obuf[3]
    t_copies = []
    for k, device in enumerate((partner, over, cross)):
        copy = remote(tsum, tbuf.at[k], t_send.at[k], t_recv.at[k], device)
        copy.start()
        t_copies.append(copy)
    for copy in t_copies:
        copy.wait_recv()
    gs_out[...] = (tsum[...] + tbuf[0] + tbuf[1] + tbuf[2])[:, :416]

    keep.wait()
    for h, count in ((0, 31), (1, 32)):
        returned = rbuf.at[0, pl.ds(0, count)]
        remote(returned, returned, r_send.at[h], r_recv.at[h], partner).wait()
    left = jnp.zeros((256, 128), f32)
    right = jnp.zeros((256, 128), f32)
    gate = jnp.zeros((256, 128), f32)
    for h in range(2):
        got = rb[h].astype(f32)
        lo = got[:, :8].reshape(256, 256)
        hi = got[:, 8:].reshape(256, 256)
        left += tn(lo.astype(bf16), onehot[...])
        right += tn(hi.astype(bf16), onehot[...])
        gate += hi[:, 128:]
    gt[0:256] = left.astype(bf16)
    gt[256:416] = right[:160].astype(bf16)
    gates_out = jnp.zeros((8, 128), f32)
    for k in range(32):
        rows8 = gate[8 * k : 8 * k + 8]
        gates_out = jnp.where(lane == k, rows8[:, 32:33] + rows8[:, 33:34], gates_out)
    gg[...] = gates_out[:, :32] / gates32

    def all_sent(q):
        for g in range(8):
            arrived(q, g).wait_send()
            forth(q, g).wait_send()
            back(q, g).wait_send()
            onward(q, g).wait_send()
            for block in range(4):
                to_partner(q, block, g).wait_send()

    by_core(all_sent)
    for copy in w_copies + t_copies + g_copies + swaps:
        copy.wait_send()
    for h in range(2):
        for copy in via[h] + alone[h] + joint[h] + gate_copies[h]:
            copy.wait_send()
        for pair_of in c_copies[h]:
            for copy in pair_of:
                copy.wait_send()
    for copy in g_copies[3:]:
        copy.wait_recv()
    for copy in stay[1:]:
        copy.wait()


DMA = pltpu.SemaphoreType.DMA


def struct(*shape, dtype=bf16):
    return jax.ShapeDtypeStruct(shape, dtype)


def settle(*refs):
    ins, outs, held, sems = refs[:6], refs[6:12], refs[12:18], refs[18]
    first = [pltpu.make_async_copy(ins[k], held[k], sems.at[0, k]) for k in range(6)]
    then = [pltpu.make_async_copy(held[k], outs[k], sems.at[1, k]) for k in range(6)]
    for copy in first:
        copy.start()
    for k in range(6):
        first[k].wait()
        then[k].start()
    for copy in then:
        copy.wait()


def local(tokens, grad_out, picks, gates, w_in, w_out, scale_in, scale_out):
    shapes = (
        struct(416, 128),
        struct(8, 32, dtype=f32),
        struct(416, 1024),
        struct(416, 1024),
        struct(4, 1, 256, dtype=f32),
        struct(1, 416, dtype=f32),
    )
    results = pl.pallas_call(
        kernel,
        out_shape=shapes,
        in_specs=[ANY, ANY, VMEM, VMEM, ANY, ANY, VMEM, VMEM],
        out_specs=(VMEM, VMEM, ANY, ANY, VMEM, VMEM),
        scratch_shapes=[
            pltpu.VMEM((128, D), bf16),
            pltpu.VMEM((128, D), bf16),
            pltpu.VMEM((256, 128), bf16),
            pltpu.VMEM((32, 16, HALF), bf16),
            pltpu.VMEM((32, 16, D - HALF), bf16),
            pltpu.VMEM((4, 32, 16, HALF), bf16),
            pltpu.VMEM((4, 32, 16, D - HALF), bf16),
            pltpu.VMEM((4, 416, 256), bf16),
            pltpu.VMEM((4, 416, 256), bf16),
            pltpu.VMEM((4, 1, 416), f32),
            pltpu.VMEM((D, 256), bf16),
            pltpu.VMEM((D, 256), f32),
            pltpu.VMEM((D, 256), bf16),
            pltpu.VMEM((D, 256), f32),
            pltpu.VMEM((D, 128), f32),
            pltpu.VMEM((D, 256), f32),
            pltpu.VMEM((D, 256), f32),
            pltpu.VMEM((4, 256, D), bf16),
            pltpu.VMEM((4, 256, D), bf16),
            pltpu.VMEM((4, 256, 256), bf16),
            pltpu.VMEM((4, 256, 256), bf16),
            pltpu.VMEM((4, 416, 256), bf16),
            pltpu.VMEM((4, 416, 256), bf16),
            pltpu.VMEM((1, 256), f32),
            pltpu.VMEM((4, 1, 512), f32),
            pltpu.VMEM((2, 4, 2, 64, D), bf16),
            pltpu.VMEM((2, 4, 8, 128), f32),
            pltpu.VMEM((2, 4, 64, D), bf16),
            pltpu.VMEM((2, 4, 8, 128), f32),
            pltpu.VMEM((2, 3, 64, D), bf16),
            pltpu.VMEM((2, 3, 8, 128), f32),
            pltpu.VMEM((2, 2, 32, D), bf16),
            pltpu.VMEM((2, 2, 64, D), bf16),
            pltpu.VMEM((2, 3, 8, 128), f32),
            pltpu.VMEM((2, 2, 2, 8, 16, 256), bf16),
            pltpu.VMEM((2, 32, 16, 256), bf16),
            pltpu.VMEM((2, 32, 16, 256), bf16),
            pltpu.VMEM((4, 1, 512), f32),
            pltpu.VMEM((3, 1, 512), f32),
            pltpu.VMEM((1, 512), f32),
            DMA((11,)),
            DMA((3, 3)), DMA((3, 3)),
            DMA((8,)), DMA((8,)),
            DMA((2, 8)), DMA((2, 8)),
            DMA((8,)), DMA((8,)),
            DMA((4, 8)), DMA((4, 8)),
            DMA((2, 2, 4)), DMA((2, 2, 4)),
            DMA((2, 9)), DMA((2, 9)),
            DMA((4, 3)), DMA((4, 3)),
            DMA((4,)), DMA((4,)),
            DMA((3,)), DMA((3,)),
        ],
        compiler_params=pltpu.CompilerParams(
            collective_id=0, has_side_effects=True, vmem_limit_bytes=58 * MIB
        ),
        name="moe_backward",
    )(
        tokens, grad_out, picks[0].T, gates[0].T, w_in[0], w_out[0].T, scale_in, scale_out,
    )
    gt, gg, gw_in, gw_out, gs_in, gs_out = pl.pallas_call(
        settle,
        out_shape=shapes,
        in_specs=[ANY] * 6,
        out_specs=(ANY,) * 6,
        scratch_shapes=[pltpu.VMEM(o.shape, o.dtype) for o in shapes] + [DMA((2, 6))],
        name="settle",
    )(*results)
    return gt.T, gg.T[None], gw_in[None], gw_out.T[None], gs_in.reshape(1, 1024), gs_out


def solution(mesh):
    placed = (
        P(("expert", "dp"), None),
        P(("expert", "dp"), None),
        P(("expert", "dp"), None, None),
        P(("expert", "dp"), None, None),
        P("expert", "dp", "tensor"),
        P("expert", "tensor", "dp"),
        P("expert", "tensor"),
        P("expert", "dp"),
    )
    return jax.shard_map(
        local,
        mesh=mesh,
        in_specs=placed,
        out_specs=(
            P(("expert", "dp"), "tensor"),
            P(("expert", "dp"), None, None),
            P("expert", "dp", "tensor"),
            P("expert", "tensor", "dp"),
            P("expert", "tensor"),
            P("expert", "dp"),
        ),
        check_vma=False,
    )
```
